128 devices in a mesh: dp: 64 (over z, y_lo, x, core), mp: 2 (over y_hi).
Axes of the slice: x: 4, y: 4 (y_hi: 2, y_lo: 2; y = y_hi * 2 + y_lo), z: 4, core: 2. Of those that a mesh axis runs over, the one named last changes fastest.
Arguments:
- img_emb: bfloat16 [16384, 1792], P('dp'), may hold values from -4 to 4
- txt_emb: bfloat16 [16384, 1792], P('dp'), may hold values from -4 to 4
- pair_ids: int32 [16384], P('dp'), may hold values from 0 to 16383, as said below
- log_scale: float32 [1], replicated, may hold values from 2.45 to 2.6
- bias: float32 [1], replicated, may hold values from -9.5 to -9
Outputs:
- grad_image: bfloat16 [16384, 1792], P(('dp', 'mp'))
- grad_text: bfloat16 [16384, 1792], P(('dp', 'mp'))
- loss: float32 [1], replicated
The draws below stay inside these ranges and needn't reach their ends.
Inputs may be any that keep to these rules, and one draw needn't show every extreme that they name: `pair_ids`: rows with equal ids are positives of each other; every row is a positive of its own row.
All inputs are finite; a program needn't handle non-finite values.
Results may differ from the reference program's by a relative error of at most 0.0054.
Values may be sent and summed in bfloat16 or wider, within the bound.
No kernel may reach another device: no remote copies, remote signals or barrier semaphores. Data moves between devices by JAX's collectives and lax.ppermute only.
A program may use at most 192 MiB of HBM per device.

```python
import math
import jax
import jax.numpy as jnp
from jax import lax

E = 1792
TOKENS = 16384


cluster_total = 16


topic_share = 0.3


def pair_groups(key):
    order = jax.random.permutation(jax.random.fold_in(key, 101), TOKENS).astype(jnp.int32)
    lottery = jax.random.randint(jax.random.fold_in(key, 102), (TOKENS,), 0, 16)
    place = order % 4
    joins = (lottery == 0) & (place >= 1) & (place <= 2)
    return jnp.where(joins, order - place, order).astype(jnp.int32)


def shared_rows(key, share_top, share_low):
    ids = pair_groups(key)
    first = jnp.take(jax.random.randint(jax.random.fold_in(key, 111), (TOKENS,), 0, cluster_total), ids)
    second = jnp.take(jax.random.randint(jax.random.fold_in(key, 112), (TOKENS,), 0, cluster_total), ids)
    centres = jax.random.normal(jax.random.fold_in(key, 113), (cluster_total, E), jnp.float32)
    weight_one = jnp.take(jax.random.normal(jax.random.fold_in(key, 114), (TOKENS,), jnp.float32), ids)
    weight_two = jnp.take(jax.random.normal(jax.random.fold_in(key, 115), (TOKENS,), jnp.float32), ids)
    content = jnp.take(jax.random.normal(jax.random.fold_in(key, 116), (TOKENS, E), jnp.float32), ids, axis=0)
    topic = (weight_one[:, None] * jnp.take(centres, first, axis=0) + weight_two[:, None] * jnp.take(centres, second, axis=0)) * jnp.sqrt(0.5)
    fraction = jnp.arange(TOKENS).astype(jnp.float32) / (TOKENS - 1)
    content_share = jnp.clip(share_top + (share_low - share_top) * fraction, 0.0, share_top)[:, None]
    shared = jnp.sqrt(topic_share) * topic + jnp.sqrt(content_share) * content
    noise_weight = jnp.sqrt(jnp.maximum(1.0 - topic_share - content_share, 0.01))
    return (shared, noise_weight)


def tower_rows(key, salt):
    shared, noise_weight = shared_rows(key, 0.55, 0.0)
    key = jax.random.fold_in(key, salt)
    noise = jax.random.normal(jax.random.fold_in(key, 2), (TOKENS, E), jnp.float32)
    scales = jnp.exp(jax.random.uniform(jax.random.fold_in(key, 3), (TOKENS, 1), jnp.float32, -0.69, 0.69))
    rows = shared + noise_weight * noise
    return jnp.clip(0.5 * scales * rows, -4.0, 4.0).astype(jnp.bfloat16)


def draw_img_emb(key, part):
    return tower_rows(key, 1)


def draw_txt_emb(key, part):
    return tower_rows(key, 5)


def draw_pair_ids(key, part):
    return pair_groups(key)


def setup_inputs(seed: int = 0) -> dict:
    arg_keys = jax.random.split(jax.random.key(seed), 6)
    img_emb = draw_img_emb(jax.random.fold_in(arg_keys[5], 71), 0)
    txt_emb = draw_txt_emb(jax.random.fold_in(arg_keys[5], 71), 0)
    pair_ids = draw_pair_ids(jax.random.fold_in(arg_keys[5], 71), 0)
    log_scale = jnp.clip(jax.random.uniform(arg_keys[3], (1,), jnp.float32, 2.45, 2.6), 2.45, 2.6)
    bias = jnp.clip(jax.random.uniform(arg_keys[4], (1,), jnp.float32, -9.5, -9.0), -9.5, -9.0)
    return dict(img_emb=img_emb, txt_emb=txt_emb, pair_ids=pair_ids, log_scale=log_scale, bias=bias)


EPS = 1e-06

def unit_rows(raw):
    values = raw.astype(jnp.float32)
    row_norm = jnp.sqrt(lax.optimization_barrier(jnp.sum(values * values, axis=1, keepdims=True)) + EPS)
    return (values / row_norm, row_norm)

def pair_terms(left, left_ids, right, right_ids, temper, offset):
    logits = temper * jnp.dot(left, right.T, preferred_element_type=jnp.float32) + offset
    signs = jnp.where(left_ids[:, None] == right_ids[None, :], 1.0, -1.0).astype(logits.dtype)
    pair_coef = (-signs * jax.nn.sigmoid(-signs * logits) * temper).astype(jnp.bfloat16)
    loss_part = jnp.sum(jnp.logaddexp(jnp.zeros_like(logits), -signs * logits))
    return (pair_coef, loss_part)

def unit_backward(unit_grad, unit, row_norm):
    inner = lax.optimization_barrier(jnp.sum(unit * unit_grad, axis=1, keepdims=True))
    return ((unit_grad - unit * inner) / row_norm).astype(jnp.bfloat16)

def reference(img_emb, txt_emb, pair_ids, log_scale, bias):
    image_unit, image_norm = unit_rows(img_emb)
    text_unit, text_norm = unit_rows(txt_emb)
    image_bf = image_unit.astype(jnp.bfloat16)
    text_bf = text_unit.astype(jnp.bfloat16)
    temper = jnp.exp(log_scale[0])
    offset = bias[0]
    block_rows = math.gcd(TOKENS, 512)
    blocks = TOKENS // block_rows
    image_blocks = image_bf.reshape(blocks, block_rows, E)
    id_blocks = pair_ids.reshape(blocks, block_rows)

    def step(carry, inputs):
        text_grad, loss_sum = carry
        block_image, block_ids = inputs
        pair_coef, loss_part = pair_terms(block_image, block_ids, text_bf, pair_ids, temper, offset)
        image_grad = jnp.dot(pair_coef, text_bf, preferred_element_type=jnp.float32)
        text_grad = text_grad + jnp.dot(pair_coef.T, block_image, preferred_element_type=jnp.float32).astype(text_grad.dtype)
        return ((text_grad, loss_sum + loss_part.astype(loss_sum.dtype)), image_grad)
    start = (jnp.zeros((TOKENS, E), image_unit.dtype), jnp.zeros((), image_unit.dtype))
    (text_grad, loss_sum), image_grads = lax.scan(step, start, (image_blocks, id_blocks))
    image_grad = image_grads.reshape(TOKENS, E)
    grad_image = unit_backward(image_grad, image_unit, image_norm)
    grad_text = unit_backward(text_grad, text_unit, text_norm)
    loss = (loss_sum / TOKENS).reshape(1).astype(jnp.float32)
    return (grad_image, grad_text, loss)
```

```python
import functools

import jax
import jax.numpy as jnp
from jax import lax
from jax.experimental import pallas as pl
from jax.experimental.pallas import tpu as pltpu
from jax.sharding import Mesh
from jax.sharding import PartitionSpec as P

EPS = 1e-06
E = 1792
EX = E + 128
ROWS = 256
HALF = ROWS // 2
LOG2E = 1.4426950408889634
VMEM = 56 << 20
f32 = jnp.float32
bf16 = jnp.bfloat16
AXES = ("z", "yl", "x", "c", "yh")
SIZES = (4, 2, 4, 2, 2)
NT = (((1,), (1,)), ((), ()))
NN = (((1,), (0,)), ((), ()))
TN = (((0,), (0,)), ((), ()))


def dot(a, b, dims):
    return lax.dot_general(a, b, dims, preferred_element_type=f32)


def payload(rows, id_row):
    values = rows.astype(f32)
    scale = lax.rsqrt(jnp.sum(values * values, axis=1, keepdims=True) + EPS)
    return (values * scale).astype(bf16)


def unit_kernel(pos_ref, img_ref, txt_ref, ids_ref, i_ref, t_ref, ty_ref):
    n = ROWS
    ids = ids_ref[...]
    eye = lax.broadcasted_iota(jnp.int32, (n, n), 0) == lax.broadcasted_iota(jnp.int32, (n, n), 1)
    hi = jnp.sum(jnp.where(eye, (ids >> 7).astype(f32), 0.0), axis=1, keepdims=True)
    lo = jnp.sum(jnp.where(eye, (ids & 127).astype(f32), 0.0), axis=1, keepdims=True)
    lane = lax.broadcasted_iota(jnp.int32, (n, 128), 1)
    tag = jnp.where(lane == 0, hi, jnp.where(lane == 1, lo, 0.0))
    i_ref[:, :E] = payload(img_ref[...], None)
    i_ref[:, E:] = tag.astype(bf16)
    yh = pos_ref[0]
    other = pos_ref[1]
    lower, upper = tag[:HALF], tag[HALF:]

    def half(which, out_ref):
        start = pl.multiple_of(which * HALF, HALF)
        out_ref[:, :E] = payload(txt_ref[pl.ds(start, HALF), :], None)
        out_ref[:, E:] = jnp.where(which == 0, lower, upper).astype(bf16)

    half(yh, t_ref)
    half(other, ty_ref)


def unit_rows(pos, img, txt, ids):
    vm = pl.BlockSpec(memory_space=pltpu.VMEM)
    return pl.pallas_call(
        unit_kernel,
        in_specs=[pl.BlockSpec(memory_space=pltpu.SMEM), vm, vm, vm],
        out_specs=[vm, vm, vm],
        out_shape=[
            jax.ShapeDtypeStruct((ROWS, EX), bf16),
            jax.ShapeDtypeStruct((HALF, EX), bf16),
            jax.ShapeDtypeStruct((HALF, EX), bf16),
        ],
        compiler_params=pltpu.CompilerParams(vmem_limit_bytes=VMEM),
        cost_estimate=pl.CostEstimate(flops=4 * ROWS * E, bytes_accessed=4 * ROWS * E * 2, transcendentals=0),
    )(pos, img, txt, ids.reshape(1, ROWS))


def id_row(tags):
    lane = lax.broadcasted_iota(jnp.int32, (8, 128), 1)
    pick = jnp.where(lane == 0, 128.0, jnp.where(lane == 1, 1.0, 0.0)).astype(bf16)
    return dot(pick, tags, NT)


def id_col(tags):
    parts = tags[:, :2].astype(f32)
    return parts[:, 0:1] * 128.0 + parts[:, 1:2]


def pair_terms(products, same, temper, scale, shift):
    t = products * scale + shift
    e = jnp.exp2(jnp.where(same, -t, t))
    u = 1.0 + e
    r = pltpu.reciprocal(u, approx=True)
    r = r * (2.0 - u * r)
    coef = (jnp.where(same, -temper, temper) * (e * r)).astype(bf16)
    loss = jnp.log(u) + (e - (u - 1.0)) * r
    return coef, loss


def pairs_kernel(offsets_i, offsets_t, cols, *refs):
    n_i, n_t = len(offsets_i), len(offsets_t)
    sc = refs[0]
    i_in, t_in = refs[1 : 1 + n_i], refs[1 + n_i : 1 + n_i + n_t]
    sib_ref, own_ref, gt_ref, loss_ref, iv, tv, acc, lacc, trow, isem, tsem = refs[1 + n_i + n_t :]
    k = pl.program_id(0)
    rows_t = tv.shape[0]

    @pl.when(k == 0)
    def _():
        for ref, off in zip(t_in, offsets_t):
            pltpu.make_async_copy(ref, tv.at[pl.ds(off, ref.shape[0])], tsem).start()
        for ref, off in zip(i_in, offsets_i):
            pltpu.make_async_copy(ref, iv.at[pl.ds(off, ref.shape[0])], isem.at[off // ROWS]).start()
        lacc[...] = jnp.zeros_like(lacc)
        acc[...] = jnp.zeros_like(acc)
        pltpu.make_async_copy(tv, tv, tsem).wait()
        trow[...] = id_row(tv[:, E:])

    block = iv.at[pl.ds(pl.multiple_of(k * ROWS, ROWS), ROWS)]
    pltpu.make_async_copy(block, block, isem.at[k]).wait()
    temper, scale, shift = sc[0], sc[1], sc[2]
    images = block[:, :E]
    column = id_col(block[:, E:])
    coefs = []
    for j in range(0, rows_t, cols):
        products = dot(images, tv[j : j + cols, :E], NT)
        coef, loss = pair_terms(products, column == trow[0:1, j : j + cols], temper, scale, shift)
        lacc[...] += jnp.sum(loss.reshape(ROWS // 8, 8, cols), axis=0)
        coefs.append(coef)
    coef = jnp.concatenate(coefs, axis=1)
    grad = dot(coef, tv[:, :E], NN).astype(bf16)

    @pl.when(k < 4)
    def _():
        sib_ref[...] = grad

    @pl.when(k >= 4)
    def _():
        own_ref[...] = grad

    acc[...] += dot(coef, images, TN)

    @pl.when(k == 7)
    def _():
        gt_ref[...] = acc[...].astype(bf16)
        loss_ref[...] = lacc[...]


def pairs(scalars, images, texts, cols=256):
    def offsets(pieces):
        out, at = [], 0
        for piece in pieces:
            out.append(at)
            at += piece.shape[0]
        return out, at

    off_i, rows_i = offsets(images)
    off_t, rows_t = offsets(texts)
    anywhere = pl.BlockSpec(memory_space=pl.ANY)
    return pl.pallas_call(
        functools.partial(pairs_kernel, off_i, off_t, cols),
        grid=(rows_i // ROWS,),
        in_specs=[pl.BlockSpec(memory_space=pltpu.SMEM)] + [anywhere] * (len(images) + len(texts)),
        out_specs=[
            pl.BlockSpec((ROWS, E), lambda k: (jnp.minimum(k, 3), 0)),
            pl.BlockSpec((ROWS, E), lambda k: (jnp.maximum(k - 4, 0), 0)),
            pl.BlockSpec((rows_t, E), lambda k: (0, 0)),
            pl.BlockSpec((8, cols), lambda k: (0, 0)),
        ],
        out_shape=[
            jax.ShapeDtypeStruct((rows_i // 2, E), bf16),
            jax.ShapeDtypeStruct((rows_i // 2, E), bf16),
            jax.ShapeDtypeStruct((rows_t, E), bf16),
            jax.ShapeDtypeStruct((8, cols), f32),
        ],
        scratch_shapes=[
            pltpu.VMEM((rows_i, EX), bf16),
            pltpu.VMEM((rows_t, EX), bf16),
            pltpu.VMEM((rows_t, E), f32),
            pltpu.VMEM((8, cols), f32),
            pltpu.VMEM((8, rows_t), f32),
            pltpu.SemaphoreType.DMA((rows_i // ROWS,)),
            pltpu.SemaphoreType.DMA,
        ],
        compiler_params=pltpu.CompilerParams(vmem_limit_bytes=VMEM),
        cost_estimate=pl.CostEstimate(
            flops=6 * rows_i * rows_t * E, bytes_accessed=2 * (2 * rows_i + 2 * rows_t) * E, transcendentals=0
        ),
    )(scalars, *images, *texts)


def backward(raw, grad):
    values = raw.astype(f32)
    inverse = lax.rsqrt(jnp.sum(values * values, axis=1, keepdims=True) + EPS)
    unit = values * inverse
    inner = jnp.sum(unit * grad, axis=1, keepdims=True)
    return ((grad - unit * inner) * inverse).astype(bf16)


def last_kernel(pos_ref, img_ref, txt_ref, i_ref, ir_ref, t_ref, tr_ref, gi_ref, gt_ref):
    rows = pl.ds(pl.multiple_of(pos_ref[0] * HALF, HALF), HALF)
    gi_ref[...] = backward(img_ref[rows, :], i_ref[rows, :] + ir_ref[...].astype(f32))
    gt_ref[...] = backward(txt_ref[rows, :], t_ref[...] + tr_ref[...].astype(f32))


def last_step(pos, img, txt, i_sum, i_recv, t_sum, t_recv):
    vm = pl.BlockSpec(memory_space=pltpu.VMEM)
    return pl.pallas_call(
        last_kernel,
        in_specs=[pl.BlockSpec(memory_space=pltpu.SMEM)] + [vm] * 6,
        out_specs=[vm, vm],
        out_shape=[jax.ShapeDtypeStruct((HALF, E), bf16)] * 2,
        compiler_params=pltpu.CompilerParams(vmem_limit_bytes=VMEM),
    )(pos, img, txt, i_sum, i_recv, t_sum, t_recv)


def shifted(value, axis, by):
    n = SIZES[AXES.index(axis)]
    return lax.ppermute(value, axis, [(i, (i + by) % n) for i in range(n)])


def swapped(value, axis, bit=1):
    n = SIZES[AXES.index(axis)]
    return lax.ppermute(value, axis, [(i, i ^ bit) for i in range(n)])


def cross_y(value):
    pairs_of = []
    for yl in range(2):
        for c in range(2):
            for yh in range(2):
                source = (yl * 2 + c) * 2 + yh
                target = ((1 - yl) * 2 + c) * 2 + (yh ^ c)
                pairs_of.append((source, target))
    return lax.ppermute(value, ("yl", "c", "yh"), pairs_of)


def add(*parts):
    return functools.reduce(lambda a, b: a + b, [p.astype(f32) for p in parts])


def reduce_ring(axis, down, up, far, own):
    half = far.shape[0] // 2
    from_low = shifted(far[:half], axis, 1)
    from_high = shifted(far[half:], axis, -1)
    up = jnp.concatenate([add(up[:half], from_low).astype(bf16), up[half:]], axis=0)
    down = jnp.concatenate([down[:half], add(down[half:], from_high).astype(bf16)], axis=0)
    got_low = shifted(up, axis, 1)
    got_high = shifted(down, axis, -1)
    return add(own, got_low, got_high)


def local(img_emb, txt_emb, pair_ids, log_scale, bias):
    yh, c = lax.axis_index("yh"), lax.axis_index("c")
    pos = jnp.stack([yh, yh ^ c]).astype(jnp.int32)
    temper = jnp.exp(log_scale[0])
    scalars = jnp.stack([temper, temper * LOG2E, bias[0] * LOG2E])
    i_own, t_own, t_cross = unit_rows(pos, img_emb, txt_emb, pair_ids)
    i_low, i_high = shifted(i_own, "z", 1), shifted(i_own, "z", -1)
    t_yl = cross_y(t_cross)
    t_low, t_high = shifted(t_own, "x", 1), shifted(t_own, "x", -1)
    ty_low, ty_high = shifted(t_yl, "x", 1), shifted(t_yl, "x", -1)
    i_far = (shifted(i_low[:HALF], "z", 1), shifted(i_high[HALF:], "z", -1))
    q = HALF // 2
    t_far = (shifted(t_low[:q], "x", 1), shifted(t_high[q:], "x", -1))
    ty_far = (shifted(ty_low[:q], "x", 1), shifted(ty_high[q:], "x", -1))
    mine = (i_low, i_high, *i_far, i_own)
    theirs = tuple(swapped(piece, "c") for piece in mine)
    texts = (t_low, ty_low, t_high, ty_high, *t_far, *ty_far, t_own, t_yl)
    sib, own, gt, loss_part = pairs(scalars, theirs + mine, texts)
    total = jnp.broadcast_to(jnp.sum(loss_part), (8, 128))
    for axis, bit in (("c", 1), ("z", 1), ("z", 2), ("x", 1), ("x", 2), ("yl", 1), ("yh", 1)):
        total = total + swapped(total, axis, bit)
    got = swapped(sib, "c")
    sums = add(own, got)
    part = [sums[i * ROWS : (i + 1) * ROWS] for i in range(4)]
    i_sum = reduce_ring("z", part[0].astype(bf16), part[1].astype(bf16), part[2].astype(bf16), part[3])
    i_send = lax.dynamic_slice_in_dim(i_sum, (1 - yh) * HALF, HALF, 0).astype(bf16)
    i_recv = swapped(i_send, "yh")
    part = [gt[i * ROWS : (i + 1) * ROWS] for i in range(4)]
    t_sum = reduce_ring("x", *part)
    t_recv = swapped(t_sum[HALF:].astype(bf16), "yl")
    grad_image, grad_text = last_step(pos, img_emb, txt_emb, i_sum, i_recv, t_sum[:HALF], t_recv)
    loss = (total[0, :1] / (64 * ROWS)).reshape(1)
    return (grad_image, grad_text, loss)


def solution(mesh):
    ring = Mesh(mesh.devices.reshape(SIZES), AXES)
    group = ("z", "yl", "x", "c")
    return jax.shard_map(
        local,
        mesh=ring,
        in_specs=(P(group, None), P(group, None), P(group), P(), P()),
        out_specs=(P(AXES, None), P(AXES, None), P()),
        check_vma=False,
    )
```

```python
import functools

import jax
import jax.numpy as jnp
from jax import lax
from jax.experimental import pallas as pl
from jax.experimental.pallas import tpu as pltpu
from jax.sharding import Mesh
from jax.sharding import PartitionSpec as P

EPS = 1e-06
E = 1792
EX = E + 128
ROWS = 256
HALF = ROWS // 2
LOG2E = 1.4426950408889634
VMEM = 56 << 20
f32 = jnp.float32
bf16 = jnp.bfloat16
AXES = ("z", "yl", "x", "c", "yh")
SIZES = (4, 2, 4, 2, 2)
NT = (((1,), (1,)), ((), ()))
NN = (((1,), (0,)), ((), ()))
TN = (((0,), (0,)), ((), ()))


def dot(a, b, dims):
    return lax.dot_general(a, b, dims, preferred_element_type=f32)


def tags_of(ids):
    n = ROWS
    eye = lax.broadcasted_iota(jnp.int32, (n, n), 0) == lax.broadcasted_iota(jnp.int32, (n, n), 1)
    hi = jnp.sum(jnp.where(eye, (ids >> 7).astype(f32), 0.0), axis=1, keepdims=True)
    lo = jnp.sum(jnp.where(eye, (ids & 127).astype(f32), 0.0), axis=1, keepdims=True)
    lane = lax.broadcasted_iota(jnp.int32, (n, 128), 1)
    return jnp.where(lane == 0, hi, jnp.where(lane == 1, lo, 0.0)).astype(bf16)


def unit(rows):
    values = rows.astype(f32)
    return (values * lax.rsqrt(jnp.sum(values * values, axis=1, keepdims=True) + EPS)).astype(bf16)


def text_kernel(pos_ref, txt_ref, ids_ref, own_ref, cross_ref, tags_ref):
    tags_ref[...] = tags_of(ids_ref[...])
    for which, out_ref in ((pos_ref[1], cross_ref), (pos_ref[0], own_ref)):
        rows = pl.ds(pl.multiple_of(which * HALF, HALF), HALF)
        out_ref[:, :E] = unit(txt_ref[rows, :])
        out_ref[:, E:] = tags_ref[rows, :]


def image_kernel(img_ref, tags_ref, out_ref):
    out_ref[:, :E] = unit(img_ref[...])
    out_ref[:, E:] = tags_ref[...]


VM = pl.BlockSpec(memory_space=pltpu.VMEM)
SM = pl.BlockSpec(memory_space=pltpu.SMEM)


def kernel_call(body, ins, outs, scratch=(), ties=(), aliases={}, limit=8 << 20, flops=0):
    specs = [SM if x.ndim == 1 else VM for x in ins] + [pl.BlockSpec(memory_space=pl.ANY)] * len(ties)
    return pl.pallas_call(
        body,
        in_specs=specs,
        out_specs=[VM] * len(outs),
        out_shape=[jax.ShapeDtypeStruct(*o) for o in outs],
        scratch_shapes=list(scratch),
        input_output_aliases=dict(aliases),
        compiler_params=pltpu.CompilerParams(vmem_limit_bytes=limit),
        cost_estimate=pl.CostEstimate(flops=0, bytes_accessed=0, transcendentals=0),
    )(*ins, *ties)


def id_row(tags):
    lane = lax.broadcasted_iota(jnp.int32, (8, 128), 1)
    pick = jnp.where(lane == 0, 128.0, jnp.where(lane == 1, 1.0, 0.0)).astype(bf16)
    return dot(pick, tags, NT)


def id_col(tags):
    parts = tags[:, :2].astype(f32)
    return parts[:, 0:1] * 128.0 + parts[:, 1:2]


def pair_terms(products, same, temper, scale, shift):
    t = products * scale + shift
    e = jnp.exp2(jnp.where(same, -t, t))
    u = 1.0 + e
    r = pltpu.reciprocal(u, approx=True)
    r = r * (2.0 - u * r)
    coef = (jnp.where(same, -temper, temper) * (e * r)).astype(bf16)
    loss = jnp.log(u) + (e - (u - 1.0)) * r
    return coef, loss


def logits_kernel(rows, cols, chunks, n_i, n_t, held, *refs):
    refs = list(refs)
    sc = refs.pop(0)
    i_in, t_in = refs[:n_i], refs[n_i : n_i + n_t]
    refs = refs[n_i + n_t + held :]
    i_buf, t_buf, coef_buf, loss_ref, trow, i_sem, t_sem = refs
    temper, scale, shift = sc[0], sc[1], sc[2]
    copies = []
    for ref, at in zip(t_in, cols):
        copies.append(pltpu.make_async_copy(ref, t_buf.at[pl.ds(at * ROWS, ROWS)], t_sem.at[len(copies)]))
    for k, (ref, at) in enumerate(zip(i_in, rows)):
        copies.append(pltpu.make_async_copy(ref, i_buf.at[pl.ds(at * ROWS, ROWS)], i_sem.at[k]))
    for copy in copies:
        copy.start()
    for copy in copies:
        copy.wait()
    loss_ref[...] = jnp.zeros_like(loss_ref)
    for first, count, blocks in chunks:
        for j in blocks:
            trow[j] = id_row(t_buf[j * ROWS : (j + 1) * ROWS, E:])

        def step(k, carry):
            here = pl.ds(pl.multiple_of(k * ROWS, ROWS), ROWS)
            images = i_buf[here, :E]
            column = id_col(i_buf[here, E:])
            for j in blocks:
                there = slice(j * ROWS, (j + 1) * ROWS)
                products = dot(images, t_buf[there, :E], NT)
                coef, loss = pair_terms(products, column == trow[j, 0:1], temper, scale, shift)
                coef_buf[here, there] = coef
                loss_ref[...] += jnp.sum(loss.reshape(ROWS // 8, 8, ROWS), axis=0)
            return carry

        lax.fori_loop(first, first + count, step, 0)


BLOCK = 2 * ROWS * ROWS * E
I_BUF = ((8 * ROWS, EX), bf16)
T_BUF = ((4 * ROWS, EX), bf16)
COEFS = ((8 * ROWS, 4 * ROWS), bf16)
LOSS = ((8, ROWS), f32)


def logits(scalars, images, texts, chunks, buffers=(), ties=()):
    rows, images = tuple(images), tuple(images.values())
    cols, texts = tuple(texts), tuple(texts.values())
    n_i, n_t = len(images), len(texts)
    body = functools.partial(logits_kernel, rows, cols, chunks, n_i, n_t, len(buffers) + len(ties))
    base = 1 + n_i + n_t
    return kernel_call(
        body,
        (scalars, *images, *texts, *buffers),
        [I_BUF, T_BUF, COEFS, LOSS],
        scratch=[
            pltpu.VMEM((4, 8, ROWS), f32),
            pltpu.SemaphoreType.DMA((max(n_i, 1),)),
            pltpu.SemaphoreType.DMA((max(n_t, 1),)),
        ],
        ties=ties,
        aliases={base + i: i for i in range(len(buffers))},
        limit=16 << 20,
        flops=BLOCK * sum(2 * count * len(blocks) for _, count, blocks in chunks),
    )


def image_grads_kernel(blocks, losses, ties, coef_ref, t_buf, *refs):
    outs = refs[losses + ties :]
    for out_ref, k in zip(outs, blocks):
        out_ref[:ROWS, :] = dot(coef_ref[k * ROWS : (k + 1) * ROWS, :], t_buf[:, :E], NN).astype(bf16)
    if losses:
        put(outs[0], jnp.sum(sum(r[...] for r in refs[:losses])))


def text_grads_kernel(blocks, ties, coef_ref, i_buf, *refs):
    for out_ref, k in zip(refs[ties:], blocks):
        out_ref[...] = dot(coef_ref[:, k * ROWS : (k + 1) * ROWS], i_buf[:, :E], TN).astype(bf16)


def image_grads(blocks, coefs, buffer, losses=(), ties=()):
    first = ((ROWS + 16 if losses else ROWS, E), bf16)
    return kernel_call(
        functools.partial(image_grads_kernel, blocks, len(losses), len(ties)),
        (coefs, buffer, *losses),
        [first] + [((ROWS, E), bf16)] * (len(blocks) - 1),
        ties=ties,
        limit=16 << 20,
        flops=len(blocks) * BLOCK * 4,
    )


def text_grads(blocks, coefs, buffer, ties=()):
    return kernel_call(
        functools.partial(text_grads_kernel, blocks, len(ties)),
        (coefs, buffer),
        [((ROWS, E), bf16)] * len(blocks),
        ties=ties,
        limit=16 << 20,
        flops=len(blocks) * BLOCK * 8,
    )


def sum_kernel(a_ref, b_ref, *refs):
    refs[-1][...] = (a_ref[...].astype(f32) + b_ref[...].astype(f32)).astype(refs[-1].dtype)


def plus(a, b, ties=()):
    return kernel_call(sum_kernel, (a, b), [(a.shape, a.dtype)], ties=ties)[0]


def far_kernel(own_ref, got_ref, *refs):
    losses, (out_ref, loss_ref) = refs[:3], refs[-2:]
    out_ref[:ROWS, :] = (own_ref[...].astype(f32) + got_ref[:ROWS, :].astype(f32)).astype(bf16)
    loss = jnp.sum(sum(r[...] for r in losses)) + take(got_ref)
    loss_ref[...] = jnp.full((8, 128), loss, f32)
    put(out_ref, loss)


def stack_kernel(at_ref, a_ref, b_ref, *refs):
    n = a_ref.shape[0]
    out_ref = refs[-1]
    out_ref[pl.ds(pl.multiple_of(at_ref[0] * n, n), n), :] = a_ref[...]
    out_ref[pl.ds(pl.multiple_of((1 - at_ref[0]) * n, n), n), :] = b_ref[...]


def stacked(at, a, b, ties=()):
    return kernel_call(stack_kernel, (at, a, b), [((2 * a.shape[0], a.shape[1]), bf16)], ties=ties)[0]


def copy_kernel(in_ref, *refs):
    refs[-1][...] = in_ref[...]


def after(value, *ties):
    return kernel_call(copy_kernel, (value,), [(value.shape, value.dtype)], ties=ties)[0]


def put(ref, number):
    lane = lax.broadcasted_iota(jnp.int32, (16, 128), 1)
    rest = jnp.full((16, 128), number, f32)
    parts = []
    for _ in range(3):
        parts.append(rest.astype(bf16).astype(f32))
        rest = rest - parts[-1]
    value = jnp.where(lane == 0, parts[0], jnp.where(lane == 1, parts[1], jnp.where(lane == 2, parts[2], 0.0)))
    ref[ROWS:, :128] = value.astype(bf16)
    ref[ROWS:, 128:] = jnp.zeros((16, E - 128), bf16)


def take(ref):
    lane = lax.broadcasted_iota(jnp.int32, (16, 128), 1)
    row = lax.broadcasted_iota(jnp.int32, (16, 128), 0)
    return jnp.sum(jnp.where((lane < 3) & (row == 0), ref[ROWS:, :128].astype(f32), 0.0))


def near_kernel(parts, losses, *refs):
    out_ref = refs[-1]
    out_ref[:ROWS, :] = sum(r[:ROWS, :].astype(f32) for r in refs[:parts]).astype(bf16)
    if losses:
        loss = refs[parts][0, 0]
        put(out_ref, loss + take(refs[parts - 1]) if refs[parts - 1].shape[0] > ROWS else loss)


def near(parts, loss=(), ties=()):
    shape = (ROWS + 16 if loss else ROWS, E)
    return kernel_call(
        functools.partial(near_kernel, len(parts), len(loss)), (*parts, *loss), [(shape, bf16)], ties=ties
    )[0]


def split_kernel(n, losses, which_ref, *refs):
    keep_ref, send_ref = refs[-3:-1] if losses else refs[-2:]
    for half, out_ref in ((which_ref[0], keep_ref), (1 - which_ref[0], send_ref)):
        rows = pl.ds(pl.multiple_of(half * HALF, HALF), HALF)
        out_ref[...] = sum(r[rows, :].astype(f32) for r in refs[:n]).astype(out_ref.dtype)
    if losses:
        refs[-1][...] = refs[n][...] + take(refs[n - 2]) + take(refs[n - 1])


def split(which, parts, sent=(), ties=()):
    return kernel_call(
        functools.partial(split_kernel, len(parts), len(sent)),
        (which, *parts, *sent),
        [((HALF, E), f32), ((HALF, E), bf16)] + [((8, 128), f32)] * len(sent),
        ties=ties,
    )


def backward(raw, grad):
    values = raw.astype(f32)
    inverse = lax.rsqrt(jnp.sum(values * values, axis=1, keepdims=True) + EPS)
    unit_values = values * inverse
    inner = jnp.sum(unit_values * grad, axis=1, keepdims=True)
    return ((grad - unit_values * inner) * inverse).astype(bf16)


def last_kernel(pos_ref, img_ref, txt_ref, i_ref, ir_ref, t_ref, tr_ref, gi_ref, gt_ref):
    rows = pl.ds(pl.multiple_of(pos_ref[0] * HALF, HALF), HALF)
    gi_ref[...] = backward(img_ref[rows, :], i_ref[...] + ir_ref[...].astype(f32))
    gt_ref[...] = backward(txt_ref[rows, :], t_ref[...] + tr_ref[...].astype(f32))


def ring(axis, by):
    n = SIZES[AXES.index(axis)]
    return [(i, (i + by) % n) for i in range(n)]


def both_ways(value, axis):
    return lax.ppermute(value, axis, ring(axis, 1)), lax.ppermute(value, axis, ring(axis, -1))


def by_core(value, axis, by=1):
    n = SIZES[AXES.index(axis)]
    perm = [(i * 2 + c, (i + (1 - 2 * c) * by) % n * 2 + c) for i in range(n) for c in range(2)]
    return lax.ppermute(value, (axis, "c"), perm)


def swapped(value, axis, bit=1):
    n = SIZES[AXES.index(axis)]
    return lax.ppermute(value, axis, [(i, i ^ bit) for i in range(n)])


def cross_y(value):
    perm = []
    for yl in range(2):
        for c in range(2):
            for yh in range(2):
                perm.append(((yl * 2 + c) * 2 + yh, ((1 - yl) * 2 + c) * 2 + (yh ^ c)))
    return lax.ppermute(value, ("yl", "c", "yh"), perm)


def local(img_emb, txt_emb, pair_ids, log_scale, bias):
    yh, c = lax.axis_index("yh"), lax.axis_index("c")
    zero = jnp.zeros((1,), jnp.int32)
    pos = jnp.stack([yh, yh ^ c]).astype(jnp.int32)
    temper = jnp.exp(log_scale[0])
    scalars = jnp.stack([temper, temper * LOG2E, bias[0] * LOG2E])
    tagged = ((HALF, EX), bf16)
    t_own, t_cross, tags = kernel_call(
        text_kernel, (pos, txt_emb, pair_ids.reshape(1, ROWS)), [tagged, tagged, ((ROWS, 128), bf16)]
    )
    (i_own,) = kernel_call(image_kernel, (img_emb, tags), [((ROWS, EX), bf16)])
    t_yl = cross_y(t_cross)
    i_one = by_core(i_own, "z")
    i_own_s = after(swapped(i_own, "c"), i_one)
    t_own = stacked(zero, t_own, t_yl, ties=(i_one,))
    i_one_s = by_core(i_own_s, "z")
    t_one = by_core(t_own, "x")
    t_one_s = by_core(swapped(t_own, "c"), "x")
    i_far = by_core(i_one, "z")
    t_far = by_core(t_one, "x")
    i_two, i_two_s = swapped(i_one_s, "c"), swapped(i_one, "c")
    t_two = swapped(t_one_s, "c")
    i_far_s = swapped(i_far, "c")
    *buffers, loss_a = logits(
        scalars,
        {0: i_own, 1: i_own_s, 2: i_one, 3: i_one_s, 4: i_far},
        {0: t_own, 1: t_one},
        [(0, 5, (0, 1))],
    )
    *buffers, loss_b = logits(
        scalars, {5: i_far_s, 6: i_two, 7: i_two_s}, {2: t_two}, [(5, 3, (0, 1, 2)), (0, 5, (2,))], buffers
    )
    *buffers, loss_c = logits(scalars, {}, {3: t_far}, [(0, 8, (3,))], buffers)
    i_buf, t_buf, coefs = buffers
    losses = (loss_a, loss_b, loss_c)
    (t_far,) = text_grads((3,), coefs, i_buf)
    t_got = by_core(t_far, "x")
    far_s, far = image_grads((5, 4), coefs, t_buf, losses, ties=(t_far,))
    (t_one,) = text_grads((1,), coefs, i_buf, ties=(far,))
    z_far, loss = kernel_call(
        far_kernel, (far, swapped(far_s, "c"), *losses), [((ROWS + 16, E), bf16), ((8, 128), f32)], ties=(t_one,)
    )
    z_got = by_core(z_far, "z")
    t_from_one = by_core(t_one, "x", -1)
    two_s, one = image_grads((7, 2), coefs, t_buf, ties=(z_far,))
    one_s, two = image_grads((3, 6), coefs, t_buf, ties=(one,))
    (t_two,) = text_grads((2,), coefs, i_buf, ties=(two,))
    z_one = near((one, swapped(two_s, "c")), (loss,), ties=(t_two,))
    z_from_one = by_core(z_one, "z", -1)
    t_two = near((t_two, t_got), ties=(z_one,))
    t_from_two = by_core(t_two, "x")
    z_two = near((two, swapped(one_s, "c"), z_got), (loss,), ties=(t_two,))
    z_from_two = by_core(z_two, "z")
    own_s, own = image_grads((1, 0), coefs, t_buf, ties=(z_two,))
    got_own = swapped(own_s, "c")
    (t_own,) = text_grads((0,), coefs, i_buf, ties=(own,))
    t_keep, t_send = split(zero, (t_own, t_from_one, t_from_two))
    t_recv = swapped(t_send, "yl")
    i_keep, i_send, loss = split(pos[:1], (own, got_own, z_from_one, z_from_two), (loss,), ties=(t_send,))
    i_recv = swapped(i_send, "yh")
    for axis, bit in (("x", 1), ("x", 2), ("yl", 1), ("yh", 1)):
        loss = plus(loss, swapped(loss, axis, bit))
    grad_image, grad_text = kernel_call(
        last_kernel, (pos, img_emb, txt_emb, i_keep, i_recv, t_keep, t_recv), [((HALF, E), bf16)] * 2
    )
    return (grad_image, grad_text, loss[0, :1] / (64 * ROWS))


def solution(mesh):
    fine = Mesh(mesh.devices.reshape(SIZES), AXES)
    group = ("z", "yl", "x", "c")
    return jax.shard_map(
        local,
        mesh=fine,
        in_specs=(P(group, None), P(group, None), P(group), P(), P()),
        out_specs=(P(AXES, None), P(AXES, None), P()),
        check_vma=False,
    )
```

```python
import functools

import jax
import jax.numpy as jnp
from jax import lax
from jax.experimental import pallas as pl
from jax.experimental.pallas import tpu as pltpu
from jax.sharding import Mesh
from jax.sharding import PartitionSpec as P

EPS = 1e-06
E = 1792
EX = E + 128
ROWS = 256
HALF = ROWS // 2
LOG2E = 1.4426950408889634
VMEM = 56 << 20
f32 = jnp.float32
bf16 = jnp.bfloat16
AXES = ("z", "yl", "x", "c", "yh")
SIZES = (4, 2, 4, 2, 2)
NT = (((1,), (1,)), ((), ()))
NN = (((1,), (0,)), ((), ()))
TN = (((0,), (0,)), ((), ()))


def dot(a, b, dims):
    return lax.dot_general(a, b, dims, preferred_element_type=f32)


def tags_of(ids):
    n = ROWS
    eye = lax.broadcasted_iota(jnp.int32, (n, n), 0) == lax.broadcasted_iota(jnp.int32, (n, n), 1)
    hi = jnp.sum(jnp.where(eye, (ids >> 7).astype(f32), 0.0), axis=1, keepdims=True)
    lo = jnp.sum(jnp.where(eye, (ids & 127).astype(f32), 0.0), axis=1, keepdims=True)
    lane = lax.broadcasted_iota(jnp.int32, (n, 128), 1)
    return jnp.where(lane == 0, hi, jnp.where(lane == 1, lo, 0.0)).astype(bf16)


def unit(rows):
    values = rows.astype(f32)
    return (values * lax.rsqrt(jnp.sum(values * values, axis=1, keepdims=True) + EPS)).astype(bf16)


def text_kernel(pos_ref, core_ref, scalars_ref, txt_ref, ids_ref, own_ref, tags_ref):
    del core_ref, scalars_ref
    tags_ref[...] = tags_of(ids_ref[...])
    rows = pl.ds(pl.multiple_of(pos_ref[0] * HALF, HALF), HALF)
    own_ref[:, :E] = unit(txt_ref[rows, :])
    own_ref[:, E:] = tags_ref[rows, :]


def image_kernel(img_ref, tags_ref, out_ref):
    out_ref[:, :E] = unit(img_ref[...])
    out_ref[:, E:] = tags_ref[...]


VM = pl.BlockSpec(memory_space=pltpu.VMEM)
SM = pl.BlockSpec(memory_space=pltpu.SMEM)


def kernel_call(body, ins, outs, scratch=(), ties=(), aliases={}, limit=6 << 20):
    specs = [SM if x.ndim == 1 else VM for x in ins] + [pl.BlockSpec(memory_space=pl.ANY)] * len(ties)
    return pl.pallas_call(
        body,
        in_specs=specs,
        out_specs=[VM] * len(outs),
        out_shape=[jax.ShapeDtypeStruct(*o) for o in outs],
        scratch_shapes=list(scratch),
        input_output_aliases=dict(aliases),
        compiler_params=pltpu.CompilerParams(vmem_limit_bytes=limit),
        cost_estimate=pl.CostEstimate(flops=0, bytes_accessed=0, transcendentals=0),
    )(*ins, *ties)


def id_row(tags):
    lane = lax.broadcasted_iota(jnp.int32, (8, 128), 1)
    pick = jnp.where(lane == 0, 128.0, jnp.where(lane == 1, 1.0, 0.0)).astype(bf16)
    return dot(pick, tags, NT)


def id_col(tags):
    parts = tags[:, :2].astype(f32)
    return parts[:, 0:1] * 128.0 + parts[:, 1:2]


def pair_terms(products, same, temper, scale, shift):
    t = products * scale + shift
    e = jnp.exp2(jnp.where(same, -t, t))
    u = 1.0 + e
    r = pltpu.reciprocal(u, approx=True)
    r = r * (2.0 - u * r)
    coef = (jnp.where(same, -temper, temper) * (e * r)).astype(bf16)
    loss = jnp.log(u) + (e - (u - 1.0)) * r
    return coef, loss


def logits_kernel(n_i, n_t, old_i, old_t, *refs):
    refs = list(refs)
    sc = refs.pop(0)
    new_i, new_t = refs[:n_i], refs[n_i : n_i + n_t]
    refs = refs[n_i + n_t :]
    had_i, had_t = refs[:old_i], refs[old_i : old_i + old_t]
    outs, (coef_ref, loss_ref, trow, sem) = refs[old_i + old_t : -4], refs[-4:]
    temper, scale, shift = sc[0], sc[1], sc[2]
    rows, cols, copies = [], [], []
    for pieces, blocks in ((new_i, rows), (new_t, cols)):
        if not pieces:
            continue
        out_ref, at = outs[len(outs) - (1 if pieces is new_t else len(outs))], 0
        for ref in pieces:
            n = ref.shape[0]
            copy = pltpu.make_async_copy(ref, out_ref.at[pl.ds(at, n)], sem.at[len(copies)])
            copy.start()
            copies.append((copy, n == ROWS))
            if n == ROWS:
                blocks.append(ref)
            elif at % ROWS == 0:
                blocks.append(out_ref.at[pl.ds(at, ROWS)])
            at += n
    for whole, blocks in ((had_i, rows), (had_t, cols)):
        for ref in whole:
            blocks += [ref.at[pl.ds(k, ROWS)] for k in range(0, ref.shape[0], ROWS)]
    for copy, late in copies:
        if not late:
            copy.wait()
    loss_ref[...] = jnp.zeros_like(loss_ref)
    for j, text in enumerate(cols):
        trow[j] = id_row(text[:, E:])
    for k, image in enumerate(rows):
        column = id_col(image[:, E:])
        for j, text in enumerate(cols):
            products = dot(image[:, :E], text[:, :E], NT)
            coef, loss = pair_terms(products, column == trow[j, 0:1], temper, scale, shift)
            coef_ref[k * ROWS : (k + 1) * ROWS, j * ROWS : (j + 1) * ROWS] = coef
            loss_ref[...] += jnp.sum(loss.reshape(ROWS // 8, 8, ROWS), axis=0)
    for copy, late in copies:
        if late:
            copy.wait()


def logits(scalars, new_i=(), new_t=(), old_i=(), old_t=(), ties=()):
    assert not ties
    total = [sum(x.shape[0] for x in group) for group in (new_i, new_t, old_i, old_t)]
    rows, cols = total[0] + total[2], total[1] + total[3]
    return kernel_call(
        functools.partial(logits_kernel, len(new_i), len(new_t), len(old_i), len(old_t)),
        (scalars, *new_i, *new_t, *old_i, *old_t),
        [((n, EX), bf16) for n in total[:2] if n] + [((rows, cols), bf16), ((8, ROWS), f32)],
        scratch=[pltpu.VMEM((cols // ROWS, 8, ROWS), f32), pltpu.SemaphoreType.DMA((len(new_i) + len(new_t),))],
        limit=10 << 20,
    )


def block(core_ref, k):
    start = jnp.where(core_ref[0] == 0, k[0], k[1]) if isinstance(k, tuple) else k
    return pl.ds(pl.multiple_of(start * ROWS, ROWS), ROWS)


def image_grads_kernel(blocks, parts, losses, ties, core_ref, *refs):
    coefs, texts = refs[:parts], refs[parts : 2 * parts]
    losses, outs = refs[2 * parts : 2 * parts + losses], refs[2 * parts + losses + ties :]
    for out_ref, k in zip(outs, blocks):
        rows = block(core_ref, k)
        at, grad = 0, None
        for n, text in enumerate(texts):
            coef = coefs[n][rows, :] if coefs[n].shape[1] == text.shape[0] else coefs[n][rows, at : at + text.shape[0]]
            part = dot(coef, text[:, :E], NN)
            grad = part if grad is None else grad + part
            at += text.shape[0]
        out_ref[:ROWS, :] = grad.astype(bf16)
    if losses:
        put(outs[0], jnp.sum(sum(r[...] for r in losses)))


def text_grads_kernel(blocks, parts, ties, core_ref, *refs):
    coefs, images = refs[:parts], refs[parts : 2 * parts]
    for out_ref, ks in zip(refs[2 * parts + ties :], blocks):
        sums = [dot(c[:, block(core_ref, k)], i[:, :E], TN) for c, i, k in zip(coefs, images, ks)]
        out_ref[...] = sum(sums[1:], sums[0]).astype(bf16)


def image_grads(core, blocks, coefs, texts, losses=(), ties=()):
    first = ((ROWS + 16 if losses else ROWS, E), bf16)
    return kernel_call(
        functools.partial(image_grads_kernel, blocks, len(texts), len(losses), len(ties)),
        (core, *coefs, *texts, *losses),
        [first] + [((ROWS, E), bf16)] * (len(blocks) - 1),
        ties=ties,
        limit=10 << 20,
    )


def text_grads(core, blocks, coefs, images, ties=()):
    return kernel_call(
        functools.partial(text_grads_kernel, blocks, len(images), len(ties)),
        (core, *coefs, *images),
        [((ROWS, E), bf16)] * len(blocks),
        ties=ties,
        limit=10 << 20,
    )


def sum_kernel(*refs):
    refs[-1][...] = sum(r[...] for r in refs[:-1])


def sum_of(*parts):
    return kernel_call(sum_kernel, parts, [(parts[0].shape, parts[0].dtype)])[0]


def far_kernel(own_ref, got_ref, *refs):
    losses, (out_ref, loss_ref) = refs[:3], refs[-2:]
    out_ref[:ROWS, :] = (own_ref[...].astype(f32) + got_ref[:ROWS, :].astype(f32)).astype(bf16)
    loss = jnp.sum(sum(r[...] for r in losses)) + take(got_ref)
    loss_ref[...] = jnp.full((8, 128), loss, f32)
    put(out_ref, loss)


def stack_kernel(at_ref, a_ref, b_ref, *refs):
    n = a_ref.shape[0]
    out_ref = refs[-1]
    out_ref[pl.ds(pl.multiple_of(at_ref[0] * n, n), n), :] = a_ref[...]
    out_ref[pl.ds(pl.multiple_of((1 - at_ref[0]) * n, n), n), :] = b_ref[...]


def stacked(at, a, b, ties=()):
    return kernel_call(stack_kernel, (at, a, b), [((2 * a.shape[0], a.shape[1]), bf16)], ties=ties)[0]


def copy_kernel(in_ref, *refs):
    refs[-1][...] = in_ref[...]


def token_kernel(a_ref, b_ref, *refs):
    refs[-1][...] = a_ref[:8, :128].astype(f32) + b_ref[:8, :128].astype(f32)


def token(a, b, ties):
    return swapped(kernel_call(token_kernel, (a, b), [((8, 128), f32)], ties=ties)[0], "c")


def after(value, *ties):
    return kernel_call(copy_kernel, (value,), [(value.shape, value.dtype)], ties=ties)[0]


def put(ref, number):
    lane = lax.broadcasted_iota(jnp.int32, (16, 128), 1)
    rest = jnp.full((16, 128), number, f32)
    parts = []
    for _ in range(3):
        parts.append(rest.astype(bf16).astype(f32))
        rest = rest - parts[-1]
    value = jnp.where(lane == 0, parts[0], jnp.where(lane == 1, parts[1], jnp.where(lane == 2, parts[2], 0.0)))
    ref[ROWS:, :128] = value.astype(bf16)
    ref[ROWS:, 128:] = jnp.zeros((16, E - 128), bf16)


def take(ref):
    lane = lax.broadcasted_iota(jnp.int32, (16, 128), 1)
    row = lax.broadcasted_iota(jnp.int32, (16, 128), 0)
    return jnp.sum(jnp.where((lane < 3) & (row == 0), ref[ROWS:, :128].astype(f32), 0.0))


def gather_gate(t_low, t_high, i_low, i_high, t_up, t_down, i_up, i_down):
    t_up[...], t_down[...] = t_low[:HALF, :], t_high[HALF:, :]
    i_up[...], i_down[...] = i_low[:HALF, :], i_high[HALF:, :]


def near_kernel(parts, losses, *refs):
    out_ref = refs[-1]
    out_ref[:ROWS, :] = sum(r[:ROWS, :].astype(f32) for r in refs[:parts]).astype(bf16)
    if losses:
        loss = refs[parts][0, 0]
        put(out_ref, loss + take(refs[parts - 1]) if refs[parts - 1].shape[0] > ROWS else loss)


def near(parts, loss=(), ties=()):
    shape = (ROWS + 16 if loss else ROWS, E)
    return kernel_call(
        functools.partial(near_kernel, len(parts), len(loss)), (*parts, *loss), [(shape, bf16)], ties=ties
    )[0]


def text_split_kernel(*refs):
    keep_ref, send_ref = refs[-2:]
    keep_ref[...] = sum(r[:HALF, :].astype(f32) for r in refs[:3])
    send_ref[...] = sum(r[HALF:, :].astype(f32) for r in refs[:3]).astype(bf16)


def image_split_kernel(half, own, own_s, z_one, z_two, loss, *refs):
    keep_ref, send_ref, loss_ref = refs[-3:]
    for which, out_ref in ((half[0], keep_ref), (1 - half[0], send_ref)):
        rows = pl.ds(pl.multiple_of(which * HALF, HALF), HALF)
        out_ref[...] = sum(r[rows, :].astype(f32) for r in (own, own_s, z_one, z_two)).astype(out_ref.dtype)
    loss_ref[...] = loss[...] + take(z_one) + take(z_two)


def backward(raw, grad):
    values = raw.astype(f32)
    inverse = lax.rsqrt(jnp.sum(values * values, axis=1, keepdims=True) + EPS)
    unit_values = values * inverse
    inner = jnp.sum(unit_values * grad, axis=1, keepdims=True)
    return ((grad - unit_values * inner) * inverse).astype(bf16)


def last_kernel(pos_ref, img_ref, txt_ref, i_ref, ir_ref, *refs):
    t_refs, (gi_ref, gt_ref) = refs[:2], refs[2:]
    rows = pl.ds(pl.multiple_of(pos_ref[0] * HALF, HALF), HALF)
    gi_ref[...] = backward(img_ref[rows, :], i_ref[...] + ir_ref[...].astype(f32))
    gt_ref[...] = backward(txt_ref[rows, :], sum(r[...].astype(f32) for r in t_refs))


def ring(axis, by):
    n = SIZES[AXES.index(axis)]
    return [(i, (i + by) % n) for i in range(n)]


def both_ways(value, axis):
    return lax.ppermute(value, axis, ring(axis, 1)), lax.ppermute(value, axis, ring(axis, -1))


def relayed(low, high, axis):
    return lax.ppermute(low[:HALF], axis, ring(axis, 1)), lax.ppermute(high[HALF:], axis, ring(axis, -1))


def by_core(value, axis, by=1):
    n = SIZES[AXES.index(axis)]
    perm = [(i * 2 + c, (i + (1 - 2 * c) * by) % n * 2 + c) for i in range(n) for c in range(2)]
    return lax.ppermute(value, (axis, "c"), perm)


def swapped(value, axis, bit=1):
    n = SIZES[AXES.index(axis)]
    return lax.ppermute(value, axis, [(i, i ^ bit) for i in range(n)])


def cross_y(value):
    perm = []
    for yl in range(2):
        for c in range(2):
            for yh in range(2):
                perm.append(((yl * 2 + c) * 2 + yh, ((1 - yl) * 2 + c) * 2 + (yh ^ c)))
    return lax.ppermute(value, ("yl", "c", "yh"), perm)


def local(img_emb, txt_emb, pair_ids, log_scale, bias):
    yh, c = lax.axis_index("yh"), lax.axis_index("c")
    core = c.reshape(1).astype(jnp.int32)
    zero = jnp.zeros((1,), jnp.int32)
    pos = yh.reshape(1).astype(jnp.int32)
    temper = jnp.exp(log_scale[0])
    scalars = jnp.stack([temper, temper * LOG2E, bias[0] * LOG2E])
    t_own, tags = kernel_call(
        text_kernel, (pos, core, scalars, txt_emb, pair_ids.reshape(1, ROWS)), [((HALF, EX), bf16), ((ROWS, 128), bf16)]
    )
    (i_own,) = kernel_call(image_kernel, (img_emb, tags), [((ROWS, EX), bf16)])
    t_yl = cross_y(t_own)
    i_low, i_high = both_ways(i_own, "z")
    i_own_s = swapped(i_own, "c")
    t_own = stacked(zero, t_own, t_yl)
    t_low, t_high = both_ways(t_own, "x")
    t_up, t_down, i_up, i_down = kernel_call(
        gather_gate, (t_low, t_high, i_low, i_high), [((HALF, EX), bf16)] * 4
    )
    t_far = lax.ppermute(t_up, "x", ring("x", 1)), lax.ppermute(t_down, "x", ring("x", -1))
    i_far = lax.ppermute(i_up, "z", ring("z", 1)), lax.ppermute(i_down, "z", ring("z", -1))
    i_low_s, i_high_s = swapped(i_low, "c"), swapped(i_high, "c")
    i_near, t_near, p_near, loss_a = logits(
        scalars, (i_own, i_own_s, i_low, i_low_s, i_high, i_high_s), (t_own, t_low, t_high)
    )
    i_far = stacked(zero, *i_far, ties=(loss_a, *t_far))
    i_far_s = swapped(i_far, "c")
    t_far, p_cols, loss_b = logits(scalars, (), t_far, (i_near,))
    i_far, p_rows, loss_c = logits(scalars, (i_far, i_far_s), (), (), (t_near, t_far))
    losses, texts, images = (loss_a, loss_b, loss_c), (t_near, t_far), (i_near, i_far)
    far_s, far = image_grads(core, (1, 0), (p_rows, p_rows), texts, losses)
    (t_far,) = text_grads(core, ((0, 3),), (p_cols, p_rows), images, ties=(far,))
    t_got = by_core(t_far, "x")
    z_far, loss = kernel_call(
        far_kernel, (far, swapped(far_s, "c"), *losses), [((ROWS + 16, E), bf16), ((8, 128), f32)], ties=(t_far,)
    )
    z_got = by_core(z_far, "z")
    near_parts, near_texts = (p_near, p_cols), (p_near, p_rows)
    two_s, one = image_grads(core, ((5, 3), (2, 4)), near_parts, texts, ties=(z_far,))
    (t_one,) = text_grads(core, (((1, 2), (1, 2)),), near_texts, images, ties=(one,))
    t_from_one = by_core(t_one, "x", -1)
    z_one = near((one, swapped(two_s, "c")), (loss,), ties=(t_one,))
    z_from_one = by_core(z_one, "z", -1)
    one_s, two = image_grads(core, ((3, 5), (4, 2)), near_parts, texts, ties=(z_one,))
    (t_two,) = text_grads(core, (((2, 1), (2, 1)),), near_texts, images, ties=(two,))
    own_s, own = image_grads(core, (1, 0), near_parts, texts, ties=(t_two,))
    (t_own,) = text_grads(core, ((0, 0),), near_texts, images, ties=(own,))
    got_two, got_own = swapped(one_s, "c"), swapped(own_s, "c")
    there = token(z_got, t_got, (z_from_one, t_from_one, t_own))
    t_two = near((t_two, t_got), ties=(there,))
    z_two = near((two, got_two, z_got), (loss,), ties=(there, got_own))
    t_from_two, z_from_two = by_core(t_two, "x"), by_core(z_two, "z")
    half = (HALF, E)
    t_keep, t_send = kernel_call(text_split_kernel, (t_own, t_from_one, t_from_two), [(half, f32), (half, bf16)])
    i_keep, i_send, loss = kernel_call(
        image_split_kernel,
        (pos, own, got_own, z_from_one, z_from_two, loss),
        [(half, f32), (half, bf16), ((8, 128), f32)],
        ties=(t_send,),
    )
    i_recv = swapped(i_send, "yh")
    t_recv = cross_y(t_send)
    loss = sum_of(loss, *[lax.ppermute(loss, "x", ring("x", by)) for by in (1, -1, 2)])
    flips = [[(i, i ^ bits) for i in range(4)] for bits in (1, 2, 3)]
    loss = sum_of(loss, *[lax.ppermute(loss, ("yl", "yh"), perm) for perm in flips])
    grad_image, grad_text = kernel_call(
        last_kernel, (pos, img_emb, txt_emb, i_keep, i_recv, t_keep, t_recv), [((HALF, E), bf16)] * 2
    )
    return (grad_image, grad_text, loss[0, :1] / (64 * ROWS))


def solution(mesh):
    fine = Mesh(mesh.devices.reshape(SIZES), AXES)
    group = ("z", "yl", "x", "c")
    return jax.shard_map(
        local,
        mesh=fine,
        in_specs=(P(group, None), P(group, None), P(group), P(), P()),
        out_specs=(P(AXES, None), P(AXES, None), P()),
        check_vma=False,
    )
```

```python
import functools

import jax
import jax.numpy as jnp
from jax import lax
from jax.experimental import pallas as pl
from jax.experimental.pallas import tpu as pltpu
from jax.sharding import Mesh
from jax.sharding import PartitionSpec as P

EPS = 1e-06
E = 1792
EX = E + 128
ROWS = 256
HALF = ROWS // 2
LOG2E = 1.4426950408889634
VMEM = 56 << 20
f32 = jnp.float32
bf16 = jnp.bfloat16
AXES = ("z", "yl", "x", "c", "yh")
SIZES = (4, 2, 4, 2, 2)
NT = (((1,), (1,)), ((), ()))
NN = (((1,), (0,)), ((), ()))
TN = (((0,), (0,)), ((), ()))


def dot(a, b, dims):
    return lax.dot_general(a, b, dims, preferred_element_type=f32)


def tags_of(ids):
    n = ROWS
    eye = lax.broadcasted_iota(jnp.int32, (n, n), 0) == lax.broadcasted_iota(jnp.int32, (n, n), 1)
    hi = jnp.sum(jnp.where(eye, (ids >> 7).astype(f32), 0.0), axis=1, keepdims=True)
    lo = jnp.sum(jnp.where(eye, (ids & 127).astype(f32), 0.0), axis=1, keepdims=True)
    lane = lax.broadcasted_iota(jnp.int32, (n, 128), 1)
    return jnp.where(lane == 0, hi, jnp.where(lane == 1, lo, 0.0)).astype(bf16)


def unit(rows):
    values = rows.astype(f32)
    return (values * lax.rsqrt(jnp.sum(values * values, axis=1, keepdims=True) + EPS)).astype(bf16)


def text_kernel(pos_ref, core_ref, txt_ref, ids_ref, own_ref, tags_ref):
    del core_ref
    tags_ref[...] = tags_of(ids_ref[...])
    rows = pl.ds(pl.multiple_of(pos_ref[0] * HALF, HALF), HALF)
    own_ref[:, :E] = unit(txt_ref[rows, :])
    own_ref[:, E:] = tags_ref[rows, :]


def image_kernel(img_ref, tags_ref, out_ref):
    out_ref[:, :E] = unit(img_ref[...])
    out_ref[:, E:] = tags_ref[...]


VM = pl.BlockSpec(memory_space=pltpu.VMEM)
SM = pl.BlockSpec(memory_space=pltpu.SMEM)


def kernel_call(body, ins, outs, scratch=(), ties=(), aliases={}, limit=6 << 20):
    specs = [SM if x.ndim == 1 else VM for x in ins] + [pl.BlockSpec(memory_space=pl.ANY)] * len(ties)
    return pl.pallas_call(
        body,
        in_specs=specs,
        out_specs=[VM] * len(outs),
        out_shape=[jax.ShapeDtypeStruct(*o) for o in outs],
        scratch_shapes=list(scratch),
        input_output_aliases=dict(aliases),
        compiler_params=pltpu.CompilerParams(vmem_limit_bytes=limit),
        cost_estimate=pl.CostEstimate(flops=0, bytes_accessed=0, transcendentals=0),
    )(*ins, *ties)


def id_row(tags):
    lane = lax.broadcasted_iota(jnp.int32, (8, 128), 1)
    pick = jnp.where(lane == 0, 128.0, jnp.where(lane == 1, 1.0, 0.0)).astype(bf16)
    return dot(pick, tags, NT)


def id_col(tags):
    parts = tags[:, :2].astype(f32)
    return parts[:, 0:1] * 128.0 + parts[:, 1:2]


def pair_terms(products, same, temper, scale, shift):
    t = products * scale + shift
    e = jnp.exp2(jnp.where(same, -t, t))
    u = 1.0 + e
    r = pltpu.reciprocal(u, approx=True)
    r = r * (2.0 - u * r)
    coef = (jnp.where(same, -temper, temper) * (e * r)).astype(bf16)
    loss = jnp.log(u) + (e - (u - 1.0)) * r
    return coef, loss


def logits_kernel(n_i, n_t, old_i, old_t, *refs):
    refs = list(refs)
    sc = refs.pop(0)
    new_i, new_t = refs[:n_i], refs[n_i : n_i + n_t]
    refs = refs[n_i + n_t :]
    had_i, had_t = refs[:old_i], refs[old_i : old_i + old_t]
    outs, (coef_ref, loss_ref, trow, i_sem, t_sem) = refs[old_i + old_t : -5], refs[-5:]
    temper, scale, shift = sc[0], sc[1], sc[2]
    rows = outs[0] if new_i else had_i[0]
    for k, ref in enumerate(new_i):
        pltpu.make_async_copy(ref, rows.at[pl.ds(k * ROWS, ROWS)], i_sem.at[k]).start()
    cols, copies, at = [], [], 0
    for k, ref in enumerate(new_t):
        copy = pltpu.make_async_copy(ref, outs[-1].at[pl.ds(at, ref.shape[0])], t_sem.at[k])
        copy.start()
        if ref.shape[0] == ROWS:
            cols.append(ref)
            copies.append(copy)
        else:
            copy.wait()
            if at % ROWS:
                cols.append(outs[-1].at[pl.ds(at - at % ROWS, ROWS)])
        at += ref.shape[0]
    for ref in had_t:
        cols += [ref.at[pl.ds(k, ROWS)] for k in range(0, ref.shape[0], ROWS)]
    loss_ref[...] = jnp.zeros_like(loss_ref)
    for j, text in enumerate(cols):
        trow[j] = id_row(text[:, E:])

    def step(k, carry):
        here = pl.ds(pl.multiple_of(k * ROWS, ROWS), ROWS)
        image = rows.at[here]
        if new_i:
            pltpu.make_async_copy(image, image, i_sem.at[k]).wait()
        column = id_col(image[:, E:])
        for j, text in enumerate(cols):
            products = dot(image[:, :E], text[:, :E], NT)
            coef, loss = pair_terms(products, column == trow[j, 0:1], temper, scale, shift)
            coef_ref[here, j * ROWS : (j + 1) * ROWS] = coef
            loss_ref[...] += jnp.sum(loss.reshape(ROWS // 8, 8, ROWS), axis=0)
        return carry

    lax.fori_loop(0, coef_ref.shape[0] // ROWS, step, 0)
    for copy in copies:
        copy.wait()


def logits(scalars, new_i=(), new_t=(), old_i=(), old_t=()):
    total = [sum(x.shape[0] for x in group) for group in (new_i, new_t, old_i, old_t)]
    rows, cols = total[0] + total[2], total[1] + total[3]
    return kernel_call(
        functools.partial(logits_kernel, len(new_i), len(new_t), len(old_i), len(old_t)),
        (scalars, *new_i, *new_t, *old_i, *old_t),
        [((n, EX), bf16) for n in total[:2] if n] + [((rows, cols), bf16), ((8, ROWS), f32)],
        scratch=[pltpu.VMEM((cols // ROWS, 8, ROWS), f32), pltpu.SemaphoreType.DMA((len(new_i) or 1,)), pltpu.SemaphoreType.DMA((len(new_t) or 1,))],
        limit=10 << 20,
    )


def block(core_ref, k):
    start = jnp.where(core_ref[0] == 0, k[0], k[1]) if isinstance(k, tuple) else k
    return pl.ds(pl.multiple_of(start * ROWS, ROWS), ROWS)


def image_grads_kernel(blocks, parts, losses, ties, core_ref, *refs):
    coefs, texts = refs[:parts], refs[parts : 2 * parts]
    losses, outs = refs[2 * parts : 2 * parts + losses], refs[2 * parts + losses + ties :]
    for out_ref, k in zip(outs, blocks):
        rows = block(core_ref, k)
        at, grad = 0, None
        for n, text in enumerate(texts):
            coef = coefs[n][rows, :] if coefs[n].shape[1] == text.shape[0] else coefs[n][rows, at : at + text.shape[0]]
            part = dot(coef, text[:, :E], NN)
            grad = part if grad is None else grad + part
            at += text.shape[0]
        out_ref[:ROWS, :] = grad.astype(bf16)
    if losses:
        put(outs[0], jnp.sum(sum(r[...] for r in losses)))


def text_grads_kernel(blocks, parts, ties, core_ref, *refs):
    coefs, images = refs[:parts], refs[parts : 2 * parts]
    for out_ref, ks in zip(refs[2 * parts + ties :], blocks):
        sums = [dot(c[:, block(core_ref, k)], i[:, :E], TN) for c, i, k in zip(coefs, images, ks)]
        out_ref[...] = sum(sums[1:], sums[0]).astype(bf16)


def image_grads(core, blocks, coefs, texts, losses=(), ties=()):
    first = ((ROWS + 16 if losses else ROWS, E), bf16)
    return kernel_call(
        functools.partial(image_grads_kernel, blocks, len(texts), len(losses), len(ties)),
        (core, *coefs, *texts, *losses),
        [first] + [((ROWS, E), bf16)] * (len(blocks) - 1),
        ties=ties,
        limit=10 << 20,
    )


def text_grads(core, blocks, coefs, images, ties=()):
    return kernel_call(
        functools.partial(text_grads_kernel, blocks, len(images), len(ties)),
        (core, *coefs, *images),
        [((ROWS, E), bf16)] * len(blocks),
        ties=ties,
        limit=10 << 20,
    )


def sum_kernel(*refs):
    refs[-1][...] = sum(r[...] for r in refs[:-1])


def sum_of(*parts):
    return kernel_call(sum_kernel, parts, [(parts[0].shape, parts[0].dtype)])[0]


def far_kernel(own_ref, got_ref, *refs):
    losses, (out_ref, loss_ref) = refs[:3], refs[-2:]
    out_ref[:ROWS, :] = (own_ref[...].astype(f32) + got_ref[:ROWS, :].astype(f32)).astype(bf16)
    loss = jnp.sum(sum(r[...] for r in losses)) + take(got_ref)
    loss_ref[...] = jnp.full((8, 128), loss, f32)
    put(out_ref, loss)


def stack_kernel(at_ref, a_ref, b_ref, *refs):
    n = a_ref.shape[0]
    out_ref = refs[-1]
    out_ref[pl.ds(pl.multiple_of(at_ref[0] * n, n), n), :] = a_ref[...]
    out_ref[pl.ds(pl.multiple_of((1 - at_ref[0]) * n, n), n), :] = b_ref[...]


def stacked(at, a, b, ties=()):
    return kernel_call(stack_kernel, (at, a, b), [((2 * a.shape[0], a.shape[1]), bf16)], ties=ties)[0]


def copy_kernel(in_ref, *refs):
    refs[-1][...] = in_ref[...]


def token_kernel(a_ref, b_ref, *refs):
    refs[-1][...] = a_ref[:8, :128].astype(f32) + b_ref[:8, :128].astype(f32)


def token(a, b, ties):
    return swapped(kernel_call(token_kernel, (a, b), [((8, 128), f32)], ties=ties)[0], "c")


def after(value, *ties):
    return kernel_call(copy_kernel, (value,), [(value.shape, value.dtype)], ties=ties)[0]


def put(ref, number):
    lane = lax.broadcasted_iota(jnp.int32, (16, 128), 1)
    rest = jnp.full((16, 128), number, f32)
    parts = []
    for _ in range(3):
        parts.append(rest.astype(bf16).astype(f32))
        rest = rest - parts[-1]
    value = jnp.where(lane == 0, parts[0], jnp.where(lane == 1, parts[1], jnp.where(lane == 2, parts[2], 0.0)))
    ref[ROWS:, :128] = value.astype(bf16)
    ref[ROWS:, 128:] = jnp.zeros((16, E - 128), bf16)


def take(ref):
    lane = lax.broadcasted_iota(jnp.int32, (16, 128), 1)
    row = lax.broadcasted_iota(jnp.int32, (16, 128), 0)
    return jnp.sum(jnp.where((lane < 3) & (row == 0), ref[ROWS:, :128].astype(f32), 0.0))


def gather_gate(t_low, t_high, i_low, i_high, t_up, t_down, i_up, i_down):
    t_up[...], t_down[...] = t_low[:HALF, :], t_high[HALF:, :]
    i_up[...], i_down[...] = i_low[:HALF, :], i_high[HALF:, :]


def near_kernel(parts, losses, *refs):
    out_ref = refs[-1]
    out_ref[:ROWS, :] = sum(r[:ROWS, :].astype(f32) for r in refs[:parts]).astype(bf16)
    if losses:
        loss = refs[parts][0, 0]
        put(out_ref, loss + take(refs[parts - 1]) if refs[parts - 1].shape[0] > ROWS else loss)


def near(parts, loss=(), ties=()):
    shape = (ROWS + 16 if loss else ROWS, E)
    return kernel_call(
        functools.partial(near_kernel, len(parts), len(loss)), (*parts, *loss), [(shape, bf16)], ties=ties
    )[0]


def text_split_kernel(*refs):
    keep_ref, send_ref = refs[-2:]
    keep_ref[...] = sum(r[:HALF, :].astype(f32) for r in refs[:3])
    send_ref[...] = sum(r[HALF:, :].astype(f32) for r in refs[:3]).astype(bf16)


def image_split_kernel(half, own, own_s, z_one, z_two, loss, *refs):
    keep_ref, send_ref, loss_ref = refs[-3:]
    for which, out_ref in ((half[0], keep_ref), (1 - half[0], send_ref)):
        rows = pl.ds(pl.multiple_of(which * HALF, HALF), HALF)
        out_ref[...] = sum(r[rows, :].astype(f32) for r in (own, own_s, z_one, z_two)).astype(out_ref.dtype)
    loss_ref[...] = loss[...] + take(z_one) + take(z_two)


def backward(raw, grad):
    values = raw.astype(f32)
    inverse = lax.rsqrt(jnp.sum(values * values, axis=1, keepdims=True) + EPS)
    unit_values = values * inverse
    inner = jnp.sum(unit_values * grad, axis=1, keepdims=True)
    return ((grad - unit_values * inner) * inverse).astype(bf16)


def last_kernel(pos_ref, img_ref, txt_ref, i_ref, ir_ref, *refs):
    t_refs, (gi_ref, gt_ref) = refs[:2], refs[2:]
    rows = pl.ds(pl.multiple_of(pos_ref[0] * HALF, HALF), HALF)
    gi_ref[...] = backward(img_ref[rows, :], i_ref[...] + ir_ref[...].astype(f32))
    gt_ref[...] = backward(txt_ref[rows, :], sum(r[...].astype(f32) for r in t_refs))


def ring(axis, by):
    n = SIZES[AXES.index(axis)]
    return [(i, (i + by) % n) for i in range(n)]


def both_ways(value, axis):
    return lax.ppermute(value, axis, ring(axis, 1)), lax.ppermute(value, axis, ring(axis, -1))


def relayed(low, high, axis):
    return lax.ppermute(low[:HALF], axis, ring(axis, 1)), lax.ppermute(high[HALF:], axis, ring(axis, -1))


def by_core(value, axis, by=1):
    n = SIZES[AXES.index(axis)]
    perm = [(i * 2 + c, (i + (1 - 2 * c) * by) % n * 2 + c) for i in range(n) for c in range(2)]
    return lax.ppermute(value, (axis, "c"), perm)


def swapped(value, axis, bit=1):
    n = SIZES[AXES.index(axis)]
    return lax.ppermute(value, axis, [(i, i ^ bit) for i in range(n)])


def cross_y(value):
    perm = []
    for yl in range(2):
        for c in range(2):
            for yh in range(2):
                perm.append(((yl * 2 + c) * 2 + yh, ((1 - yl) * 2 + c) * 2 + (yh ^ c)))
    return lax.ppermute(value, ("yl", "c", "yh"), perm)


def local(img_emb, txt_emb, pair_ids, log_scale, bias):
    yh, c = lax.axis_index("yh"), lax.axis_index("c")
    core = c.reshape(1).astype(jnp.int32)
    zero = jnp.zeros((1,), jnp.int32)
    pos = yh.reshape(1).astype(jnp.int32)
    temper = jnp.exp(log_scale[0])
    scalars = jnp.stack([temper, temper * LOG2E, bias[0] * LOG2E])
    t_own, tags = kernel_call(
        text_kernel, (pos, core, txt_emb, pair_ids.reshape(1, ROWS)), [((HALF, EX), bf16), ((ROWS, 128), bf16)]
    )
    (i_own,) = kernel_call(image_kernel, (img_emb, tags), [((ROWS, EX), bf16)])
    t_yl = cross_y(t_own)
    i_low, i_high = both_ways(i_own, "z")
    i_own_s = swapped(i_own, "c")
    t_own = stacked(zero, t_own, t_yl)
    t_low, t_high = both_ways(t_own, "x")
    t_up, t_down, i_up, i_down = kernel_call(
        gather_gate, (t_low, t_high, i_low, i_high), [((HALF, EX), bf16)] * 4
    )
    t_far = lax.ppermute(t_up, "x", ring("x", 1)), lax.ppermute(t_down, "x", ring("x", -1))
    i_far = lax.ppermute(i_up, "z", ring("z", 1)), lax.ppermute(i_down, "z", ring("z", -1))
    i_low_s, i_high_s = swapped(i_low, "c"), swapped(i_high, "c")
    i_near, t_near, p_near, loss_a = logits(
        scalars, (i_own, i_own_s, i_low, i_low_s, i_high, i_high_s), (t_own, t_low, t_high)
    )
    i_far = stacked(zero, *i_far, ties=(loss_a, *t_far))
    i_far_s = swapped(i_far, "c")
    t_far, p_cols, loss_b = logits(scalars, (), t_far, (i_near,))
    i_far, p_rows, loss_c = logits(scalars, (i_far, i_far_s), (), (), (t_near, t_far))
    losses, texts, images = (loss_a, loss_b, loss_c), (t_near, t_far), (i_near, i_far)
    far_s, far = image_grads(core, (1, 0), (p_rows, p_rows), texts, losses)
    (t_far,) = text_grads(core, ((0, 3),), (p_cols, p_rows), images, ties=(far,))
    t_got = by_core(t_far, "x")
    z_far, loss = kernel_call(
        far_kernel, (far, swapped(far_s, "c"), *losses), [((ROWS + 16, E), bf16), ((8, 128), f32)], ties=(t_far,)
    )
    z_got = by_core(z_far, "z")
    near_parts, near_texts = (p_near, p_cols), (p_near, p_rows)
    two_s, one = image_grads(core, ((5, 3), (2, 4)), near_parts, texts, ties=(z_far,))
    (t_one,) = text_grads(core, (((1, 2), (1, 2)),), near_texts, images, ties=(one,))
    t_from_one = by_core(t_one, "x", -1)
    z_one = near((one, swapped(two_s, "c")), (loss,), ties=(t_one,))
    z_from_one = by_core(z_one, "z", -1)
    one_s, two = image_grads(core, ((3, 5), (4, 2)), near_parts, texts, ties=(z_one,))
    (t_two,) = text_grads(core, (((2, 1), (2, 1)),), near_texts, images, ties=(two,))
    own_s, own = image_grads(core, (1, 0), near_parts, texts, ties=(t_two,))
    (t_own,) = text_grads(core, ((0, 0),), near_texts, images, ties=(own,))
    got_two, got_own = swapped(one_s, "c"), swapped(own_s, "c")
    there = token(z_got, t_got, (z_from_one, t_from_one, t_own))
    t_two = near((t_two, t_got), ties=(there,))
    z_two = near((two, got_two, z_got), (loss,), ties=(there, got_own))
    t_from_two, z_from_two = by_core(t_two, "x"), by_core(z_two, "z")
    half = (HALF, E)
    t_keep, t_send = kernel_call(text_split_kernel, (t_own, t_from_one, t_from_two), [(half, f32), (half, bf16)])
    i_keep, i_send, loss = kernel_call(
        image_split_kernel,
        (pos, own, got_own, z_from_one, z_from_two, loss),
        [(half, f32), (half, bf16), ((8, 128), f32)],
        ties=(t_send,),
    )
    i_recv = swapped(i_send, "yh")
    t_recv = cross_y(t_send)
    loss = sum_of(loss, *[lax.ppermute(loss, "x", ring("x", by)) for by in (1, -1, 2)])
    flips = [[(i, i ^ bits) for i in range(4)] for bits in (1, 2, 3)]
    loss = sum_of(loss, *[lax.ppermute(loss, ("yl", "yh"), perm) for perm in flips])
    grad_image, grad_text = kernel_call(
        last_kernel, (pos, img_emb, txt_emb, i_keep, i_recv, t_keep, t_recv), [((HALF, E), bf16)] * 2
    )
    return (grad_image, grad_text, loss[0, :1] / (64 * ROWS))


def solution(mesh):
    fine = Mesh(mesh.devices.reshape(SIZES), AXES)
    group = ("z", "yl", "x", "c")
    return jax.shard_map(
        local,
        mesh=fine,
        in_specs=(P(group, None), P(group, None), P(group), P(), P()),
        out_specs=(P(AXES, None), P(AXES, None), P()),
        check_vma=False,
    )
```

```python
import functools

import jax
import jax.numpy as jnp
from jax import lax
from jax.experimental import pallas as pl
from jax.experimental.pallas import tpu as pltpu
from jax.sharding import Mesh
from jax.sharding import PartitionSpec as P

EPS = 1e-06
E = 1792
EX = E + 128
ROWS = 256
HALF = ROWS // 2
STEP = 2 * ROWS
LOG2E = 1.4426950408889634
VMEM = 56 << 20
f32 = jnp.float32
bf16 = jnp.bfloat16
AXES = ("z", "yl", "x", "c", "yh")
SIZES = (4, 2, 4, 2, 2)
NT = (((1,), (1,)), ((), ()))
NN = (((1,), (0,)), ((), ()))
TN = (((0,), (0,)), ((), ()))


def dot(a, b, dims):
    return lax.dot_general(a, b, dims, preferred_element_type=f32)


def tags_of(ids):
    n = ROWS
    eye = lax.broadcasted_iota(jnp.int32, (n, n), 0) == lax.broadcasted_iota(jnp.int32, (n, n), 1)
    hi = jnp.sum(jnp.where(eye, (ids >> 7).astype(f32), 0.0), axis=1, keepdims=True)
    lo = jnp.sum(jnp.where(eye, (ids & 127).astype(f32), 0.0), axis=1, keepdims=True)
    lane = lax.broadcasted_iota(jnp.int32, (n, 128), 1)
    return jnp.where(lane == 0, hi, jnp.where(lane == 1, lo, 0.0)).astype(bf16)


def unit(rows):
    values = rows.astype(f32)
    return (values * lax.rsqrt(jnp.sum(values * values, axis=1, keepdims=True) + EPS)).astype(bf16)


def text_kernel(pos_ref, core_ref, txt_ref, ids_ref, own_ref, tags_ref):
    del core_ref
    tags_ref[...] = tags_of(ids_ref[...])
    rows = pl.ds(pl.multiple_of(pos_ref[0] * HALF, HALF), HALF)
    own_ref[:, :E] = unit(txt_ref[rows, :])
    own_ref[:, E:] = tags_ref[rows, :]


def image_kernel(scalars_ref, img_ref, tags_ref, *refs):
    del scalars_ref
    out_ref = refs[-1]
    out_ref[:, :E] = unit(img_ref[...])
    out_ref[:, E:] = tags_ref[...]


VM = pl.BlockSpec(memory_space=pltpu.VMEM)
SM = pl.BlockSpec(memory_space=pltpu.SMEM)


def kernel_call(body, ins, outs, scratch=(), ties=(), aliases={}, limit=6 << 20):
    specs = [SM if x.ndim == 1 else VM for x in ins] + [pl.BlockSpec(memory_space=pl.ANY)] * len(ties)
    return pl.pallas_call(
        body,
        in_specs=specs,
        out_specs=[VM] * len(outs),
        out_shape=[jax.ShapeDtypeStruct(*o) for o in outs],
        scratch_shapes=list(scratch),
        input_output_aliases=dict(aliases),
        compiler_params=pltpu.CompilerParams(vmem_limit_bytes=limit),
        cost_estimate=pl.CostEstimate(flops=0, bytes_accessed=0, transcendentals=0),
    )(*ins, *ties)


def id_row(tags):
    lane = lax.broadcasted_iota(jnp.int32, (8, 128), 1)
    pick = jnp.where(lane == 0, 128.0, jnp.where(lane == 1, 1.0, 0.0)).astype(bf16)
    return dot(pick, tags, NT)


def id_col(tags):
    parts = tags[:, :2].astype(f32)
    return parts[:, 0:1] * 128.0 + parts[:, 1:2]


def pair_terms(products, same, temper, scale, shift):
    t = products * scale + shift
    e = jnp.exp2(jnp.where(same, -t, t))
    u = 1.0 + e
    r = pltpu.reciprocal(u, approx=True)
    r = r * (2.0 - u * r)
    coef = (jnp.where(same, -temper, temper) * (e * r)).astype(bf16)
    loss = jnp.log(u) + (e - (u - 1.0)) * r
    return coef, loss


def logits_kernel(n_i, n_t, old_i, old_t, *refs):
    refs = list(refs)
    sc = refs.pop(0)
    new_i, new_t = refs[:n_i], refs[n_i : n_i + n_t]
    refs = refs[n_i + n_t :]
    had_i, had_t = refs[:old_i], refs[old_i : old_i + old_t]
    outs, (coef_ref, loss_ref, trow, i_sem, t_sem) = refs[old_i + old_t : -5], refs[-5:]
    temper, scale, shift = sc[0], sc[1], sc[2]
    rows = outs[0] if new_i else had_i[0]
    for k, ref in enumerate(new_i):
        pltpu.make_async_copy(ref, rows.at[pl.ds(k * ROWS, ROWS)], i_sem.at[k]).start()
    cols, copies = [], []
    for k, ref in enumerate(new_t):
        copy = pltpu.make_async_copy(ref, outs[-1].at[pl.ds(k * ROWS, ROWS)], t_sem.at[k])
        copy.start()
        cols.append(ref)
        copies.append(copy)
    for ref in had_t:
        cols += [ref.at[pl.ds(k, ROWS)] for k in range(0, ref.shape[0], ROWS)]
    loss_ref[...] = jnp.zeros_like(loss_ref)
    for j, text in enumerate(cols):
        trow[j] = id_row(text[:, E:])

    def step(k, carry):
        here = pl.ds(pl.multiple_of(k * STEP, STEP), STEP)
        image = rows.at[here]
        if new_i:
            for part in range(STEP // ROWS):
                piece = image.at[pl.ds(part * ROWS, ROWS)]
                pltpu.make_async_copy(piece, piece, i_sem.at[k * (STEP // ROWS) + part]).wait()
        column = id_col(image[:, E:])
        for j, text in enumerate(cols):
            products = dot(image[:, :E], text[:, :E], NT)
            coef, loss = pair_terms(products, column == trow[j, 0:1], temper, scale, shift)
            coef_ref[here, j * ROWS : (j + 1) * ROWS] = coef
            loss_ref[...] += jnp.sum(loss.reshape(STEP // 8, 8, ROWS), axis=0)
        return carry

    lax.fori_loop(0, coef_ref.shape[0] // STEP, step, 0)
    for copy in copies:
        copy.wait()


def logits(scalars, new_i=(), new_t=(), old_i=(), old_t=()):
    total = [sum(x.shape[0] for x in group) for group in (new_i, new_t, old_i, old_t)]
    rows, cols = total[0] + total[2], total[1] + total[3]
    return kernel_call(
        functools.partial(logits_kernel, len(new_i), len(new_t), len(old_i), len(old_t)),
        (scalars, *new_i, *new_t, *old_i, *old_t),
        [((n, EX), bf16) for n in total[:2] if n] + [((rows, cols), bf16), ((8, ROWS), f32)],
        scratch=[pltpu.VMEM((cols // ROWS, 8, ROWS), f32), pltpu.SemaphoreType.DMA((len(new_i) or 1,)), pltpu.SemaphoreType.DMA((len(new_t) or 1,))],
        limit=12 << 20,
    )


def block(core_ref, k):
    start = jnp.where(core_ref[0] == 0, k[0], k[1]) if isinstance(k, tuple) else k
    return pl.ds(pl.multiple_of(start * ROWS, ROWS), ROWS)


def image_grads_kernel(blocks, parts, losses, ties, core_ref, *refs):
    coefs, texts = refs[:parts], refs[parts : 2 * parts]
    losses, outs = refs[2 * parts : 2 * parts + losses], refs[2 * parts + losses + ties :]
    for out_ref, k in zip(outs, blocks):
        rows = block(core_ref, k)
        at, grad = 0, None
        for n, text in enumerate(texts):
            coef = coefs[n][rows, :] if coefs[n].shape[1] == text.shape[0] else coefs[n][rows, at : at + text.shape[0]]
            part = dot(coef, text[:, :E], NN)
            grad = part if grad is None else grad + part
            at += text.shape[0]
        out_ref[:ROWS, :] = grad.astype(bf16)
    if losses:
        put(outs[0], jnp.sum(sum(r[...] for r in losses)))


def text_grads_kernel(blocks, parts, ties, core_ref, *refs):
    coefs, images = refs[:parts], refs[parts : 2 * parts]
    for out_ref, ks in zip(refs[2 * parts + ties :], blocks):
        sums = [dot(c[:, block(core_ref, k)], i[:, :E], TN) for c, i, k in zip(coefs, images, ks)]
        out_ref[...] = sum(sums[1:], sums[0]).astype(bf16)


def image_grads(core, blocks, coefs, texts, losses=(), ties=()):
    first = ((ROWS + 16 if losses else ROWS, E), bf16)
    return kernel_call(
        functools.partial(image_grads_kernel, blocks, len(texts), len(losses), len(ties)),
        (core, *coefs, *texts, *losses),
        [first] + [((ROWS, E), bf16)] * (len(blocks) - 1),
        ties=ties,
        limit=10 << 20,
    )


def text_grads(core, blocks, coefs, images, ties=()):
    return kernel_call(
        functools.partial(text_grads_kernel, blocks, len(images), len(ties)),
        (core, *coefs, *images),
        [((ROWS, E), bf16)] * len(blocks),
        ties=ties,
        limit=10 << 20,
    )


def sum_kernel(*refs):
    refs[-1][...] = sum(r[...] for r in refs[:-1])


def sum_of(*parts):
    return kernel_call(sum_kernel, parts, [(parts[0].shape, parts[0].dtype)])[0]


def far_kernel(own_ref, got_ref, *refs):
    losses, (out_ref, loss_ref) = refs[:3], refs[-2:]
    out_ref[...] = (own_ref[...].astype(f32) + got_ref[:ROWS, :].astype(f32)).astype(bf16)
    loss_ref[...] = jnp.full((8, 128), jnp.sum(sum(r[...] for r in losses)) + take(got_ref), f32)


def stack_kernel(at_ref, a_ref, b_ref, *refs):
    n = a_ref.shape[0]
    out_ref = refs[-1]
    out_ref[pl.ds(pl.multiple_of(at_ref[0] * n, n), n), :] = a_ref[...]
    out_ref[pl.ds(pl.multiple_of((1 - at_ref[0]) * n, n), n), :] = b_ref[...]


def stacked(at, a, b, ties=()):
    return kernel_call(stack_kernel, (at, a, b), [((2 * a.shape[0], a.shape[1]), bf16)], ties=ties)[0]


def copy_kernel(in_ref, *refs):
    refs[-1][...] = in_ref[...]


def token_kernel(a_ref, b_ref, *refs):
    refs[-1][...] = a_ref[:8, :128].astype(f32) + b_ref[:8, :128].astype(f32)


def token(a, b, ties):
    return swapped(kernel_call(token_kernel, (a, b), [((8, 128), f32)], ties=ties)[0], "c")


def after(value, *ties):
    return kernel_call(copy_kernel, (value,), [(value.shape, value.dtype)], ties=ties)[0]


def put(ref, number):
    lane = lax.broadcasted_iota(jnp.int32, (16, 128), 1)
    rest = jnp.full((16, 128), number, f32)
    parts = []
    for _ in range(3):
        parts.append(rest.astype(bf16).astype(f32))
        rest = rest - parts[-1]
    value = jnp.where(lane == 0, parts[0], jnp.where(lane == 1, parts[1], jnp.where(lane == 2, parts[2], 0.0)))
    ref[ROWS:, :128] = value.astype(bf16)
    ref[ROWS:, 128:] = jnp.zeros((16, E - 128), bf16)


def take(ref):
    lane = lax.broadcasted_iota(jnp.int32, (16, 128), 1)
    row = lax.broadcasted_iota(jnp.int32, (16, 128), 0)
    return jnp.sum(jnp.where((lane < 3) & (row == 0), ref[ROWS:, :128].astype(f32), 0.0))


def gather_gate(core, t_low, t_high, i_low, i_high, t_out, i_out):
    for k, (text, image) in enumerate(((t_low, i_low), (t_high, i_high))):

        @pl.when(core[0] == k)
        def _():
            t_out[...], i_out[...] = text[...], image[...]


def near_kernel(parts, *refs):
    refs[-1][...] = sum(r[...].astype(f32) for r in refs[:parts]).astype(bf16)


def near(parts, ties=()):
    return kernel_call(functools.partial(near_kernel, len(parts)), parts, [((ROWS, E), bf16)], ties=ties)[0]


def text_split_kernel(*refs):
    keep_ref, send_ref = refs[-2:]
    keep_ref[...] = sum(r[:HALF, :].astype(f32) for r in refs[:3])
    send_ref[...] = sum(r[HALF:, :].astype(f32) for r in refs[:3]).astype(bf16)


def image_split_kernel(half, *refs):
    keep_ref, send_ref = refs[-2:]
    for which, out_ref in ((half[0], keep_ref), (1 - half[0], send_ref)):
        rows = pl.ds(pl.multiple_of(which * HALF, HALF), HALF)
        out_ref[...] = sum(r[rows, :].astype(f32) for r in refs[:4]).astype(out_ref.dtype)


def backward(raw, grad):
    values = raw.astype(f32)
    inverse = lax.rsqrt(jnp.sum(values * values, axis=1, keepdims=True) + EPS)
    unit_values = values * inverse
    inner = jnp.sum(unit_values * grad, axis=1, keepdims=True)
    return ((grad - unit_values * inner) * inverse).astype(bf16)


def last_kernel(pos_ref, img_ref, txt_ref, i_ref, ir_ref, *refs):
    t_refs, (gi_ref, gt_ref) = refs[:2], refs[2:]
    rows = pl.ds(pl.multiple_of(pos_ref[0] * HALF, HALF), HALF)
    gi_ref[...] = backward(img_ref[rows, :], i_ref[...] + ir_ref[...].astype(f32))
    gt_ref[...] = backward(txt_ref[rows, :], sum(r[...].astype(f32) for r in t_refs))


def ring(axis, by):
    n = SIZES[AXES.index(axis)]
    return [(i, (i + by) % n) for i in range(n)]


def both_ways(value, axis):
    return lax.ppermute(value, axis, ring(axis, 1)), lax.ppermute(value, axis, ring(axis, -1))


def by_core(value, axis, by=1):
    n = SIZES[AXES.index(axis)]
    perm = [(i * 2 + c, (i + (1 - 2 * c) * by) % n * 2 + c) for i in range(n) for c in range(2)]
    return lax.ppermute(value, (axis, "c"), perm)


def swapped(value, axis, bit=1):
    n = SIZES[AXES.index(axis)]
    return lax.ppermute(value, axis, [(i, i ^ bit) for i in range(n)])


def cross_y(value):
    perm = []
    for yl in range(2):
        for c in range(2):
            for yh in range(2):
                perm.append(((yl * 2 + c) * 2 + yh, ((1 - yl) * 2 + c) * 2 + (yh ^ c)))
    return lax.ppermute(value, ("yl", "c", "yh"), perm)


def local(img_emb, txt_emb, pair_ids, log_scale, bias):
    yh, c = lax.axis_index("yh"), lax.axis_index("c")
    core = c.reshape(1).astype(jnp.int32)
    zero = jnp.zeros((1,), jnp.int32)
    pos = yh.reshape(1).astype(jnp.int32)
    temper = jnp.exp(log_scale[0])
    scalars = jnp.stack([temper, temper * LOG2E, bias[0] * LOG2E])
    t_own, tags = kernel_call(
        text_kernel, (pos, core, txt_emb, pair_ids.reshape(1, ROWS)), [((HALF, EX), bf16), ((ROWS, 128), bf16)]
    )
    t_yl = cross_y(t_own)
    (i_own,) = kernel_call(image_kernel, (scalars, img_emb, tags), [((ROWS, EX), bf16)])
    i_own = after(i_own, t_yl)
    i_low, i_high = both_ways(i_own, "z")
    i_own_s = swapped(i_own, "c")
    t_own = stacked(zero, t_own, t_yl)
    t_low, t_high = both_ways(t_own, "x")
    t_pass, i_pass = kernel_call(
        gather_gate, (core, t_low, t_high, i_low, i_high), [((ROWS, EX), bf16)] * 2
    )
    t_far, i_far = by_core(t_pass, "x"), by_core(i_pass, "z")
    i_low_s, i_high_s = swapped(i_low, "c"), swapped(i_high, "c")
    i_near, t_near, p_near, loss_a = logits(
        scalars, (i_own, i_own_s, i_low, i_low_s, i_high, i_high_s), (t_own, t_low, t_high)
    )
    i_far = after(i_far, loss_a, t_far)
    i_far_s = swapped(i_far, "c")
    t_far, p_cols, loss_b = logits(scalars, (), (t_far,), (i_near,))
    i_far, p_rows, loss_c = logits(scalars, (i_far, i_far_s), (), (), (t_near, t_far))
    losses, texts, images = (loss_a, loss_b, loss_c), (t_near, t_far), (i_near, i_far)
    far_s, far = image_grads(core, (1, 0), (p_rows, p_rows), texts, losses)
    (t_far,) = text_grads(core, ((0, 3),), (p_cols, p_rows), images, ties=(far,))
    t_got = by_core(t_far, "x")
    z_far, loss = kernel_call(
        far_kernel, (far, swapped(far_s, "c"), *losses), [((ROWS, E), bf16), ((8, 128), f32)], ties=(t_far,)
    )
    z_got = by_core(z_far, "z")
    near_parts, near_texts = (p_near, p_cols), (p_near, p_rows)
    two_s, one = image_grads(core, ((5, 3), (2, 4)), near_parts, texts, ties=(z_far,))
    (t_one,) = text_grads(core, (((1, 2), (1, 2)),), near_texts, images, ties=(one,))
    t_from_one = by_core(t_one, "x", -1)
    z_one = near((one, swapped(two_s, "c")), ties=(t_one,))
    z_from_one = by_core(z_one, "z", -1)
    one_s, two = image_grads(core, ((3, 5), (4, 2)), near_parts, texts, ties=(z_one,))
    (t_two,) = text_grads(core, (((2, 1), (2, 1)),), near_texts, images, ties=(two,))
    own_s, own = image_grads(core, (1, 0), near_parts, texts, ties=(t_two,))
    (t_own,) = text_grads(core, ((0, 0),), near_texts, images, ties=(own,))
    got_two, got_own = swapped(one_s, "c"), swapped(own_s, "c")
    there = token(z_got, t_got, (z_from_one, t_from_one, t_own))
    t_two = near((t_two, t_got), ties=(there,))
    z_two = near((two, got_two, z_got), ties=(there, got_own))
    t_from_two, z_from_two = by_core(t_two, "x"), by_core(z_two, "z")
    loss = after(loss, z_two, t_two)
    flips = [[(i, i ^ bits) for i in range(4)] for bits in (1, 2, 3)]
    loss = sum_of(loss, *[lax.ppermute(loss, ("yl", "yh"), perm) for perm in flips])
    half = (HALF, E)
    t_keep, t_send = kernel_call(
        text_split_kernel, (t_own, t_from_one, t_from_two), [(half, f32), (half, bf16)], ties=(loss,)
    )
    i_keep, i_send = kernel_call(
        image_split_kernel, (pos, own, got_own, z_from_one, z_from_two), [(half, f32), (half, bf16)], ties=(t_send,)
    )
    loss = after(loss, i_send)
    i_recv = swapped(i_send, "yh")
    t_recv = cross_y(t_send)
    for axis in ("x", "z"):
        loss = sum_of(loss, *[lax.ppermute(loss, axis, ring(axis, by)) for by in (1, -1, 2)])
    grad_image, grad_text = kernel_call(
        last_kernel, (pos, img_emb, txt_emb, i_keep, i_recv, t_keep, t_recv), [((HALF, E), bf16)] * 2
    )
    return (grad_image, grad_text, loss[0, :1] / (64 * ROWS))


def solution(mesh):
    fine = Mesh(mesh.devices.reshape(SIZES), AXES)
    group = ("z", "yl", "x", "c")
    return jax.shard_map(
        local,
        mesh=fine,
        in_specs=(P(group, None), P(group, None), P(group), P(), P()),
        out_specs=(P(AXES, None), P(AXES, None), P()),
        check_vma=False,
    )
```

```python
import functools

import jax
import jax.numpy as jnp
from jax import lax
from jax.experimental import pallas as pl
from jax.experimental.pallas import tpu as pltpu
from jax.sharding import Mesh
from jax.sharding import PartitionSpec as P

EPS = 1e-06
E = 1792
EX = E + 128
ROWS = 256
HALF = ROWS // 2
STEP = 2 * ROWS
LOG2E = 1.4426950408889634
VMEM = 56 << 20
f32 = jnp.float32
bf16 = jnp.bfloat16
AXES = ("z", "yl", "x", "c", "yh")
SIZES = (4, 2, 4, 2, 2)
NT = (((1,), (1,)), ((), ()))
NN = (((1,), (0,)), ((), ()))
TN = (((0,), (0,)), ((), ()))


def dot(a, b, dims):
    return lax.dot_general(a, b, dims, preferred_element_type=f32)


def tags_of(ids):
    n = ROWS
    eye = lax.broadcasted_iota(jnp.int32, (n, n), 0) == lax.broadcasted_iota(jnp.int32, (n, n), 1)
    hi = jnp.sum(jnp.where(eye, (ids >> 7).astype(f32), 0.0), axis=1, keepdims=True)
    lo = jnp.sum(jnp.where(eye, (ids & 127).astype(f32), 0.0), axis=1, keepdims=True)
    lane = lax.broadcasted_iota(jnp.int32, (n, 128), 1)
    return jnp.where(lane == 0, hi, jnp.where(lane == 1, lo, 0.0)).astype(bf16)


def unit(rows):
    values = rows.astype(f32)
    return (values * lax.rsqrt(jnp.sum(values * values, axis=1, keepdims=True) + EPS)).astype(bf16)


def text_kernel(pos_ref, core_ref, txt_ref, ids_ref, own_ref, tags_ref):
    del core_ref
    tags_ref[...] = tags_of(ids_ref[...])
    rows = pl.ds(pl.multiple_of(pos_ref[0] * HALF, HALF), HALF)
    own_ref[:, :E] = unit(txt_ref[rows, :])
    own_ref[:, E:] = tags_ref[rows, :]


def image_kernel(scalars_ref, img_ref, tags_ref, *refs):
    del scalars_ref
    out_ref = refs[-1]
    out_ref[:, :E] = unit(img_ref[...])
    out_ref[:, E:] = tags_ref[...]


VM = pl.BlockSpec(memory_space=pltpu.VMEM)
SM = pl.BlockSpec(memory_space=pltpu.SMEM)


def kernel_call(body, ins, outs, scratch=(), ties=(), aliases={}, limit=6 << 20):
    specs = [SM if x.ndim == 1 else VM for x in ins] + [pl.BlockSpec(memory_space=pl.ANY)] * len(ties)
    return pl.pallas_call(
        body,
        in_specs=specs,
        out_specs=[VM] * len(outs),
        out_shape=[jax.ShapeDtypeStruct(*o) for o in outs],
        scratch_shapes=list(scratch),
        input_output_aliases=dict(aliases),
        compiler_params=pltpu.CompilerParams(vmem_limit_bytes=limit),
        cost_estimate=pl.CostEstimate(flops=0, bytes_accessed=0, transcendentals=0),
    )(*ins, *ties)


def id_row(tags):
    lane = lax.broadcasted_iota(jnp.int32, (8, 128), 1)
    pick = jnp.where(lane == 0, 128.0, jnp.where(lane == 1, 1.0, 0.0)).astype(bf16)
    return dot(pick, tags, NT)


def id_col(tags):
    parts = tags[:, :2].astype(f32)
    return parts[:, 0:1] * 128.0 + parts[:, 1:2]


def pair_terms(products, same, temper, scale, shift):
    t = products * scale + shift
    e = jnp.exp2(jnp.where(same, -t, t))
    u = 1.0 + e
    r = pltpu.reciprocal(u, approx=True)
    r = r * (2.0 - u * r)
    coef = (jnp.where(same, -temper, temper) * (e * r)).astype(bf16)
    loss = jnp.log(u) + (e - (u - 1.0)) * r
    return coef, loss


def logits_kernel(n_i, n_t, old_i, old_t, *refs):
    refs = list(refs)
    sc = refs.pop(0)
    new_i, new_t = refs[:n_i], refs[n_i : n_i + n_t]
    refs = refs[n_i + n_t :]
    had_i, had_t = refs[:old_i], refs[old_i : old_i + old_t]
    outs, (coef_ref, loss_ref, trow, i_sem, t_sem) = refs[old_i + old_t : -5], refs[-5:]
    temper, scale, shift = sc[0], sc[1], sc[2]
    rows = outs[0] if new_i else had_i[0]
    for k, ref in enumerate(new_i):
        pltpu.make_async_copy(ref, rows.at[pl.ds(k * ROWS, ROWS)], i_sem.at[k]).start()
    cols, copies = [], []
    for k, ref in enumerate(new_t):
        copy = pltpu.make_async_copy(ref, outs[-1].at[pl.ds(k * ROWS, ROWS)], t_sem.at[k])
        copy.start()
        cols.append(ref)
        copies.append(copy)
    for ref in had_t:
        cols += [ref.at[pl.ds(k, ROWS)] for k in range(0, ref.shape[0], ROWS)]
    loss_ref[...] = jnp.zeros_like(loss_ref)
    for j, text in enumerate(cols):
        trow[j] = id_row(text[:, E:])

    def step(image, here):
        column = id_col(image[:, E:])
        for j, text in enumerate(cols):
            products = dot(image[:, :E], text[:, :E], NT)
            coef, loss = pair_terms(products, column == trow[j, 0:1], temper, scale, shift)
            coef_ref[here, j * ROWS : (j + 1) * ROWS] = coef
            loss_ref[...] += jnp.sum(loss.reshape(image.shape[0] // 8, 8, ROWS), axis=0)

    def copied_step(k, carry):
        here = pl.ds(pl.multiple_of(k * STEP, STEP), STEP)
        for part in range(STEP // ROWS):
            piece = rows.at[pl.ds(pl.multiple_of(k * STEP + part * ROWS, ROWS), ROWS)]
            pltpu.make_async_copy(piece, piece, i_sem.at[k * (STEP // ROWS) + part]).wait()
        step(rows.at[here], here)
        return carry

    if n_i > 2:
        lax.fori_loop(0, n_i * ROWS // STEP, copied_step, 0)
    elif n_i:
        for k, ref in enumerate(new_i):
            step(ref, pl.ds(k * ROWS, ROWS))
        for k in range(n_i):
            piece = rows.at[pl.ds(k * ROWS, ROWS)]
            pltpu.make_async_copy(piece, piece, i_sem.at[k]).wait()
    else:
        for k in range(0, rows.shape[0], STEP):
            step(rows.at[pl.ds(k, STEP)], pl.ds(k, STEP))
    for copy in copies:
        copy.wait()


def logits(scalars, new_i=(), new_t=(), old_i=(), old_t=()):
    total = [sum(x.shape[0] for x in group) for group in (new_i, new_t, old_i, old_t)]
    rows, cols = total[0] + total[2], total[1] + total[3]
    return kernel_call(
        functools.partial(logits_kernel, len(new_i), len(new_t), len(old_i), len(old_t)),
        (scalars, *new_i, *new_t, *old_i, *old_t),
        [((n, EX), bf16) for n in total[:2] if n] + [((rows, cols), bf16), ((8, ROWS), f32)],
        scratch=[pltpu.VMEM((cols // ROWS, 8, ROWS), f32), pltpu.SemaphoreType.DMA((len(new_i) or 1,)), pltpu.SemaphoreType.DMA((len(new_t) or 1,))],
        limit=12 << 20,
    )


def block(core_ref, k):
    start = jnp.where(core_ref[0] == 0, k[0], k[1]) if isinstance(k, tuple) else k
    return pl.ds(pl.multiple_of(start * ROWS, ROWS), ROWS)


def image_grads_kernel(blocks, parts, losses, ties, core_ref, *refs):
    coefs, texts = refs[:parts], refs[parts : 2 * parts]
    losses, outs = refs[2 * parts : 2 * parts + losses], refs[2 * parts + losses + ties :]
    for out_ref, k in zip(outs, blocks):
        rows = block(core_ref, k)
        at, grad = 0, None
        for n, text in enumerate(texts):
            coef = coefs[n][rows, :] if coefs[n].shape[1] == text.shape[0] else coefs[n][rows, at : at + text.shape[0]]
            part = dot(coef, text[:, :E], NN)
            grad = part if grad is None else grad + part
            at += text.shape[0]
        out_ref[:ROWS, :] = grad.astype(bf16)
    if losses:
        put(outs[0], jnp.sum(sum(r[...] for r in losses)))


def text_grads_kernel(blocks, parts, ties, core_ref, *refs):
    coefs, images = refs[:parts], refs[parts : 2 * parts]
    for out_ref, ks in zip(refs[2 * parts + ties :], blocks):
        sums = [dot(c[:, block(core_ref, k)], i[:, :E], TN) for c, i, k in zip(coefs, images, ks)]
        out_ref[...] = sum(sums[1:], sums[0]).astype(bf16)


def image_grads(core, blocks, coefs, texts, losses=(), ties=()):
    first = ((ROWS + 16 if losses else ROWS, E), bf16)
    return kernel_call(
        functools.partial(image_grads_kernel, blocks, len(texts), len(losses), len(ties)),
        (core, *coefs, *texts, *losses),
        [first] + [((ROWS, E), bf16)] * (len(blocks) - 1),
        ties=ties,
        limit=10 << 20,
    )


def text_grads(core, blocks, coefs, images, ties=()):
    return kernel_call(
        functools.partial(text_grads_kernel, blocks, len(images), len(ties)),
        (core, *coefs, *images),
        [((ROWS, E), bf16)] * len(blocks),
        ties=ties,
        limit=10 << 20,
    )


def sum_kernel(*refs):
    refs[-1][...] = sum(r[...] for r in refs[:-1])


def sum_of(*parts):
    return kernel_call(sum_kernel, parts, [(parts[0].shape, parts[0].dtype)])[0]


def far_kernel(own_ref, got_ref, *refs):
    losses, (out_ref, loss_ref) = refs[:3], refs[-2:]
    out_ref[...] = (own_ref[...].astype(f32) + got_ref[:ROWS, :].astype(f32)).astype(bf16)
    loss_ref[...] = jnp.full((8, 128), jnp.sum(sum(r[...] for r in losses)) + take(got_ref), f32)


def stack_kernel(at_ref, a_ref, b_ref, *refs):
    n = a_ref.shape[0]
    out_ref = refs[-1]
    out_ref[pl.ds(pl.multiple_of(at_ref[0] * n, n), n), :] = a_ref[...]
    out_ref[pl.ds(pl.multiple_of((1 - at_ref[0]) * n, n), n), :] = b_ref[...]


def stacked(at, a, b, ties=()):
    return kernel_call(stack_kernel, (at, a, b), [((2 * a.shape[0], a.shape[1]), bf16)], ties=ties)[0]


def copy_kernel(in_ref, *refs):
    refs[-1][...] = in_ref[...]


def token_kernel(a_ref, b_ref, *refs):
    refs[-1][...] = a_ref[:8, :128].astype(f32) + b_ref[:8, :128].astype(f32)


def token(a, b, ties):
    return swapped(kernel_call(token_kernel, (a, b), [((8, 128), f32)], ties=ties)[0], "c")


def after(value, *ties):
    return kernel_call(copy_kernel, (value,), [(value.shape, value.dtype)], ties=ties)[0]


def put(ref, number):
    lane = lax.broadcasted_iota(jnp.int32, (16, 128), 1)
    rest = jnp.full((16, 128), number, f32)
    parts = []
    for _ in range(3):
        parts.append(rest.astype(bf16).astype(f32))
        rest = rest - parts[-1]
    value = jnp.where(lane == 0, parts[0], jnp.where(lane == 1, parts[1], jnp.where(lane == 2, parts[2], 0.0)))
    ref[ROWS:, :128] = value.astype(bf16)
    ref[ROWS:, 128:] = jnp.zeros((16, E - 128), bf16)


def take(ref):
    lane = lax.broadcasted_iota(jnp.int32, (16, 128), 1)
    row = lax.broadcasted_iota(jnp.int32, (16, 128), 0)
    return jnp.sum(jnp.where((lane < 3) & (row == 0), ref[ROWS:, :128].astype(f32), 0.0))


def gather_gate(core, t_low, t_high, i_low, i_high, t_out, i_out):
    for k, (text, image) in enumerate(((t_low, i_low), (t_high, i_high))):

        @pl.when(core[0] == k)
        def _():
            t_out[...], i_out[...] = text[...], image[...]


def near_kernel(parts, *refs):
    refs[-1][...] = sum(r[...].astype(f32) for r in refs[:parts]).astype(bf16)


def near(parts, ties=()):
    return kernel_call(functools.partial(near_kernel, len(parts)), parts, [((ROWS, E), bf16)], ties=ties)[0]


def text_split_kernel(*refs):
    keep_ref, send_ref = refs[-2:]
    keep_ref[...] = sum(r[:HALF, :].astype(f32) for r in refs[:3])
    send_ref[...] = sum(r[HALF:, :].astype(f32) for r in refs[:3]).astype(bf16)


def image_split_kernel(half, *refs):
    keep_ref, send_ref = refs[-2:]
    for which, out_ref in ((half[0], keep_ref), (1 - half[0], send_ref)):
        rows = pl.ds(pl.multiple_of(which * HALF, HALF), HALF)
        out_ref[...] = sum(r[rows, :].astype(f32) for r in refs[:4]).astype(out_ref.dtype)


def backward(raw, grad):
    values = raw.astype(f32)
    inverse = lax.rsqrt(jnp.sum(values * values, axis=1, keepdims=True) + EPS)
    unit_values = values * inverse
    inner = jnp.sum(unit_values * grad, axis=1, keepdims=True)
    return ((grad - unit_values * inner) * inverse).astype(bf16)


def last_kernel(pos_ref, img_ref, txt_ref, i_ref, ir_ref, *refs):
    t_refs, (gi_ref, gt_ref) = refs[:2], refs[2:]
    rows = pl.ds(pl.multiple_of(pos_ref[0] * HALF, HALF), HALF)
    gi_ref[...] = backward(img_ref[rows, :], i_ref[...] + ir_ref[...].astype(f32))
    gt_ref[...] = backward(txt_ref[rows, :], sum(r[...].astype(f32) for r in t_refs))


def ring(axis, by):
    n = SIZES[AXES.index(axis)]
    return [(i, (i + by) % n) for i in range(n)]


def both_ways(value, axis):
    return lax.ppermute(value, axis, ring(axis, 1)), lax.ppermute(value, axis, ring(axis, -1))


def by_core(value, axis, by=1):
    n = SIZES[AXES.index(axis)]
    perm = [(i * 2 + c, (i + (1 - 2 * c) * by) % n * 2 + c) for i in range(n) for c in range(2)]
    return lax.ppermute(value, (axis, "c"), perm)


def swapped(value, axis, bit=1):
    n = SIZES[AXES.index(axis)]
    return lax.ppermute(value, axis, [(i, i ^ bit) for i in range(n)])


def cross_y(value):
    perm = []
    for yl in range(2):
        for c in range(2):
            for yh in range(2):
                perm.append(((yl * 2 + c) * 2 + yh, ((1 - yl) * 2 + c) * 2 + (yh ^ c)))
    return lax.ppermute(value, ("yl", "c", "yh"), perm)


def local(img_emb, txt_emb, pair_ids, log_scale, bias):
    yh, c = lax.axis_index("yh"), lax.axis_index("c")
    core = c.reshape(1).astype(jnp.int32)
    zero = jnp.zeros((1,), jnp.int32)
    pos = yh.reshape(1).astype(jnp.int32)
    temper = jnp.exp(log_scale[0])
    scalars = jnp.stack([temper, temper * LOG2E, bias[0] * LOG2E])
    t_own, tags = kernel_call(
        text_kernel, (pos, core, txt_emb, pair_ids.reshape(1, ROWS)), [((HALF, EX), bf16), ((ROWS, 128), bf16)]
    )
    t_yl = cross_y(t_own)
    (i_own,) = kernel_call(image_kernel, (scalars, img_emb, tags), [((ROWS, EX), bf16)])
    i_own = after(i_own, t_yl)
    i_low, i_high = both_ways(i_own, "z")
    i_own_s = swapped(i_own, "c")
    t_own = stacked(zero, t_own, t_yl)
    t_low, t_high = both_ways(t_own, "x")
    t_pass, i_pass = kernel_call(
        gather_gate, (core, t_low, t_high, i_low, i_high), [((ROWS, EX), bf16)] * 2
    )
    t_far, i_far = by_core(t_pass, "x"), by_core(i_pass, "z")
    i_low_s, i_high_s = swapped(i_low, "c"), swapped(i_high, "c")
    i_near, t_near, p_near, loss_a = logits(
        scalars, (i_own, i_own_s, i_low, i_low_s, i_high, i_high_s), (t_own, t_low, t_high)
    )
    i_far = after(i_far, loss_a, t_far)
    i_far_s = swapped(i_far, "c")
    t_far, p_cols, loss_b = logits(scalars, (), (t_far,), (i_near,))
    i_far, p_rows, loss_c = logits(scalars, (i_far, i_far_s), (), (), (t_near, t_far))
    losses, texts, images = (loss_a, loss_b, loss_c), (t_near, t_far), (i_near, i_far)
    far_s, far = image_grads(core, (1, 0), (p_rows, p_rows), texts, losses)
    (t_far,) = text_grads(core, ((0, 3),), (p_cols, p_rows), images, ties=(far,))
    t_got = by_core(t_far, "x")
    z_far, loss = kernel_call(
        far_kernel, (far, swapped(far_s, "c"), *losses), [((ROWS, E), bf16), ((8, 128), f32)], ties=(t_far,)
    )
    z_got = by_core(z_far, "z")
    near_parts, near_texts = (p_near, p_cols), (p_near, p_rows)
    two_s, one = image_grads(core, ((5, 3), (2, 4)), near_parts, texts, ties=(z_far,))
    (t_one,) = text_grads(core, (((1, 2), (1, 2)),), near_texts, images, ties=(one,))
    t_from_one = by_core(t_one, "x", -1)
    z_one = near((one, swapped(two_s, "c")), ties=(t_one,))
    z_from_one = by_core(z_one, "z", -1)
    one_s, two = image_grads(core, ((3, 5), (4, 2)), near_parts, texts, ties=(z_one,))
    (t_two,) = text_grads(core, (((2, 1), (2, 1)),), near_texts, images, ties=(two,))
    own_s, own = image_grads(core, (1, 0), near_parts, texts, ties=(t_two,))
    (t_own,) = text_grads(core, ((0, 0),), near_texts, images, ties=(own,))
    got_two, got_own = swapped(one_s, "c"), swapped(own_s, "c")
    there = token(z_got, t_got, (z_from_one, t_from_one, t_own))
    t_two = near((t_two, t_got), ties=(there,))
    z_two = near((two, got_two, z_got), ties=(there, got_own))
    t_from_two, z_from_two = by_core(t_two, "x"), by_core(z_two, "z")
    loss = after(loss, z_two, t_two)
    flips = [[(i, i ^ bits) for i in range(4)] for bits in (1, 2, 3)]
    loss = sum_of(loss, *[lax.ppermute(loss, ("yl", "yh"), perm) for perm in flips])
    half = (HALF, E)
    t_keep, t_send = kernel_call(
        text_split_kernel, (t_own, t_from_one, t_from_two), [(half, f32), (half, bf16)], ties=(loss,)
    )
    i_keep, i_send = kernel_call(
        image_split_kernel, (pos, own, got_own, z_from_one, z_from_two), [(half, f32), (half, bf16)], ties=(t_send,)
    )
    loss = after(loss, i_send)
    i_recv = swapped(i_send, "yh")
    t_recv = cross_y(t_send)
    for axis in ("x", "z"):
        loss = sum_of(loss, *[lax.ppermute(loss, axis, ring(axis, by)) for by in (1, -1, 2)])
    grad_image, grad_text = kernel_call(
        last_kernel, (pos, img_emb, txt_emb, i_keep, i_recv, t_keep, t_recv), [((HALF, E), bf16)] * 2
    )
    return (grad_image, grad_text, loss[0, :1] / (64 * ROWS))


def solution(mesh):
    fine = Mesh(mesh.devices.reshape(SIZES), AXES)
    group = ("z", "yl", "x", "c")
    return jax.shard_map(
        local,
        mesh=fine,
        in_specs=(P(group, None), P(group, None), P(group), P(), P()),
        out_specs=(P(AXES, None), P(AXES, None), P()),
        check_vma=False,
    )
```

```python
import functools

import jax
import jax.numpy as jnp
from jax import lax
from jax.experimental import pallas as pl
from jax.experimental.pallas import tpu as pltpu
from jax.sharding import Mesh
from jax.sharding import PartitionSpec as P

EPS = 1e-06
E = 1792
EX = E + 128
ROWS = 256
HALF = ROWS // 2
STEP = 2 * ROWS
LOG2E = 1.4426950408889634
VMEM = 56 << 20
f32 = jnp.float32
bf16 = jnp.bfloat16
AXES = ("z", "yl", "x", "c", "yh")
SIZES = (4, 2, 4, 2, 2)
NT = (((1,), (1,)), ((), ()))
NN = (((1,), (0,)), ((), ()))
TN = (((0,), (0,)), ((), ()))


def dot(a, b, dims):
    return lax.dot_general(a, b, dims, preferred_element_type=f32)


def tags_of(ids):
    n = ROWS
    eye = lax.broadcasted_iota(jnp.int32, (n, n), 0) == lax.broadcasted_iota(jnp.int32, (n, n), 1)
    hi = jnp.sum(jnp.where(eye, (ids >> 7).astype(f32), 0.0), axis=1, keepdims=True)
    lo = jnp.sum(jnp.where(eye, (ids & 127).astype(f32), 0.0), axis=1, keepdims=True)
    lane = lax.broadcasted_iota(jnp.int32, (n, 128), 1)
    return jnp.where(lane == 0, hi, jnp.where(lane == 1, lo, 0.0)).astype(bf16)


def unit(rows):
    values = rows.astype(f32)
    return (values * lax.rsqrt(jnp.sum(values * values, axis=1, keepdims=True) + EPS)).astype(bf16)


def text_kernel(pos_ref, core_ref, txt_ref, ids_ref, own_ref, tags_ref):
    del core_ref
    tags_ref[...] = tags_of(ids_ref[...])
    rows = pl.ds(pl.multiple_of(pos_ref[0] * HALF, HALF), HALF)
    own_ref[:, :E] = unit(txt_ref[rows, :])
    own_ref[:, E:] = tags_ref[rows, :]


def image_kernel(scalars_ref, img_ref, tags_ref, *refs):
    del scalars_ref
    out_ref = refs[-1]
    out_ref[:, :E] = unit(img_ref[...])
    out_ref[:, E:] = tags_ref[...]


VM = pl.BlockSpec(memory_space=pltpu.VMEM)
SM = pl.BlockSpec(memory_space=pltpu.SMEM)


def kernel_call(body, ins, outs, scratch=(), ties=(), aliases={}, limit=6 << 20):
    specs = [SM if x.ndim == 1 else VM for x in ins] + [pl.BlockSpec(memory_space=pl.ANY)] * len(ties)
    return pl.pallas_call(
        body,
        in_specs=specs,
        out_specs=[VM] * len(outs),
        out_shape=[jax.ShapeDtypeStruct(*o) for o in outs],
        scratch_shapes=list(scratch),
        input_output_aliases=dict(aliases),
        compiler_params=pltpu.CompilerParams(vmem_limit_bytes=limit),
        cost_estimate=pl.CostEstimate(flops=0, bytes_accessed=0, transcendentals=0),
    )(*ins, *ties)


def id_row(tags):
    lane = lax.broadcasted_iota(jnp.int32, (8, 128), 1)
    pick = jnp.where(lane == 0, 128.0, jnp.where(lane == 1, 1.0, 0.0)).astype(bf16)
    return dot(pick, tags, NT)


def id_col(tags):
    parts = tags[:, :2].astype(f32)
    return parts[:, 0:1] * 128.0 + parts[:, 1:2]


def pair_terms(products, same, temper, scale, shift):
    t = products * scale + shift
    e = jnp.exp2(jnp.where(same, -t, t))
    u = 1.0 + e
    r = pltpu.reciprocal(u, approx=True)
    r = r * (2.0 - u * r)
    coef = (jnp.where(same, -temper, temper) * (e * r)).astype(bf16)
    loss = jnp.log(u) + (e - (u - 1.0)) * r
    return coef, loss


def logits_kernel(n_i, n_t, old_i, old_t, *refs):
    refs = list(refs)
    sc = refs.pop(0)
    new_i, new_t = refs[:n_i], refs[n_i : n_i + n_t]
    refs = refs[n_i + n_t :]
    had_i, had_t = refs[:old_i], refs[old_i : old_i + old_t]
    outs, (coef_ref, loss_ref, trow, i_sem, t_sem) = refs[old_i + old_t : -5], refs[-5:]
    temper, scale, shift = sc[0], sc[1], sc[2]
    rows = outs[0] if new_i else had_i[0]
    for k, ref in enumerate(new_i):
        pltpu.make_async_copy(ref, rows.at[pl.ds(k * ROWS, ROWS)], i_sem.at[k]).start()
    cols, copies = [], []
    for k, ref in enumerate(new_t):
        copy = pltpu.make_async_copy(ref, outs[-1].at[pl.ds(k * ROWS, ROWS)], t_sem.at[k])
        copy.start()
        cols.append(ref)
        copies.append(copy)
    for ref in had_t:
        cols += [ref.at[pl.ds(k, ROWS)] for k in range(0, ref.shape[0], ROWS)]
    loss_ref[...] = jnp.zeros_like(loss_ref)
    for j, text in enumerate(cols):
        trow[j] = id_row(text[:, E:])

    def step(image, here):
        column = id_col(image[:, E:])
        for j, text in enumerate(cols):
            products = dot(image[:, :E], text[:, :E], NT)
            coef, loss = pair_terms(products, column == trow[j, 0:1], temper, scale, shift)
            coef_ref[here, j * ROWS : (j + 1) * ROWS] = coef
            loss_ref[...] += jnp.sum(loss.reshape(image.shape[0] // 8, 8, ROWS), axis=0)

    def copied_step(k, carry):
        here = pl.ds(pl.multiple_of(k * STEP, STEP), STEP)
        for part in range(STEP // ROWS):
            piece = rows.at[pl.ds(pl.multiple_of(k * STEP + part * ROWS, ROWS), ROWS)]
            pltpu.make_async_copy(piece, piece, i_sem.at[k * (STEP // ROWS) + part]).wait()
        step(rows.at[here], here)
        return carry

    if n_i > 2:
        lax.fori_loop(0, n_i * ROWS // STEP, copied_step, 0)
    elif n_i:
        for k, ref in enumerate(new_i):
            step(ref, pl.ds(k * ROWS, ROWS))
        for k in range(n_i):
            piece = rows.at[pl.ds(k * ROWS, ROWS)]
            pltpu.make_async_copy(piece, piece, i_sem.at[k]).wait()
    else:
        for k in range(0, rows.shape[0], STEP):
            step(rows.at[pl.ds(k, STEP)], pl.ds(k, STEP))
    for copy in copies:
        copy.wait()


def logits(scalars, new_i=(), new_t=(), old_i=(), old_t=()):
    total = [sum(x.shape[0] for x in group) for group in (new_i, new_t, old_i, old_t)]
    rows, cols = total[0] + total[2], total[1] + total[3]
    return kernel_call(
        functools.partial(logits_kernel, len(new_i), len(new_t), len(old_i), len(old_t)),
        (scalars, *new_i, *new_t, *old_i, *old_t),
        [((n, EX), bf16) for n in total[:2] if n] + [((rows, cols), bf16), ((8, ROWS), f32)],
        scratch=[pltpu.VMEM((cols // ROWS, 8, ROWS), f32), pltpu.SemaphoreType.DMA((len(new_i) or 1,)), pltpu.SemaphoreType.DMA((len(new_t) or 1,))],
        limit=12 << 20,
    )


def block(core_ref, k):
    start = jnp.where(core_ref[0] == 0, k[0], k[1]) if isinstance(k, tuple) else k
    return pl.ds(pl.multiple_of(start * ROWS, ROWS), ROWS)


def image_grads_kernel(blocks, parts, losses, ties, core_ref, *refs):
    coefs, texts = refs[:parts], refs[parts : 2 * parts]
    losses, outs = refs[2 * parts : 2 * parts + losses], refs[2 * parts + losses + ties :]
    for out_ref, k in zip(outs, blocks):
        rows = block(core_ref, k)
        at, grad = 0, None
        for n, text in enumerate(texts):
            coef = coefs[n][rows, :] if coefs[n].shape[1] == text.shape[0] else coefs[n][rows, at : at + text.shape[0]]
            part = dot(coef, text[:, :E], NN)
            grad = part if grad is None else grad + part
            at += text.shape[0]
        out_ref[:ROWS, :] = grad.astype(bf16)
    if losses:
        put(outs[0], jnp.sum(sum(r[...] for r in losses)))


def text_grads_kernel(blocks, parts, ties, core_ref, *refs):
    coefs, images = refs[:parts], refs[parts : 2 * parts]
    for out_ref, ks in zip(refs[2 * parts + ties :], blocks):
        sums = [dot(c[:, block(core_ref, k)], i[:, :E], TN) for c, i, k in zip(coefs, images, ks)]
        out_ref[...] = sum(sums[1:], sums[0]).astype(bf16)


def image_grads(core, blocks, coefs, texts, losses=(), ties=()):
    first = ((ROWS + 16 if losses else ROWS, E), bf16)
    return kernel_call(
        functools.partial(image_grads_kernel, blocks, len(texts), len(losses), len(ties)),
        (core, *coefs, *texts, *losses),
        [first] + [((ROWS, E), bf16)] * (len(blocks) - 1),
        ties=ties,
        limit=10 << 20,
    )


def text_grads(core, blocks, coefs, images, ties=()):
    return kernel_call(
        functools.partial(text_grads_kernel, blocks, len(images), len(ties)),
        (core, *coefs, *images),
        [((ROWS, E), bf16)] * len(blocks),
        ties=ties,
        limit=10 << 20,
    )


def sum_kernel(*refs):
    refs[-1][...] = sum(r[...] for r in refs[:-1])


def sum_of(*parts):
    return kernel_call(sum_kernel, parts, [(parts[0].shape, parts[0].dtype)])[0]


def far_kernel(own_ref, got_ref, *refs):
    losses, (out_ref, loss_ref) = refs[:3], refs[-2:]
    out_ref[...] = (own_ref[...].astype(f32) + got_ref[:ROWS, :].astype(f32)).astype(bf16)
    loss_ref[...] = jnp.full((8, 128), jnp.sum(sum(r[...] for r in losses)) + take(got_ref), f32)


def stack_kernel(at_ref, a_ref, b_ref, *refs):
    n = a_ref.shape[0]
    out_ref = refs[-1]
    out_ref[pl.ds(pl.multiple_of(at_ref[0] * n, n), n), :] = a_ref[...]
    out_ref[pl.ds(pl.multiple_of((1 - at_ref[0]) * n, n), n), :] = b_ref[...]


def stacked(at, a, b, ties=()):
    return kernel_call(stack_kernel, (at, a, b), [((2 * a.shape[0], a.shape[1]), bf16)], ties=ties)[0]


def copy_kernel(in_ref, *refs):
    refs[-1][...] = in_ref[...]


def after(value, *ties):
    return kernel_call(copy_kernel, (value,), [(value.shape, value.dtype)], ties=ties)[0]


def put(ref, number):
    lane = lax.broadcasted_iota(jnp.int32, (16, 128), 1)
    rest = jnp.full((16, 128), number, f32)
    parts = []
    for _ in range(3):
        parts.append(rest.astype(bf16).astype(f32))
        rest = rest - parts[-1]
    value = jnp.where(lane == 0, parts[0], jnp.where(lane == 1, parts[1], jnp.where(lane == 2, parts[2], 0.0)))
    ref[ROWS:, :128] = value.astype(bf16)
    ref[ROWS:, 128:] = jnp.zeros((16, E - 128), bf16)


def take(ref):
    lane = lax.broadcasted_iota(jnp.int32, (16, 128), 1)
    row = lax.broadcasted_iota(jnp.int32, (16, 128), 0)
    return jnp.sum(jnp.where((lane < 3) & (row == 0), ref[ROWS:, :128].astype(f32), 0.0))


def gather_gate(core, t_low, t_high, i_low, i_high, t_out, i_out):
    for k, (text, image) in enumerate(((t_low, i_low), (t_high, i_high))):

        @pl.when(core[0] == k)
        def _():
            t_out[...], i_out[...] = text[...], image[...]


def near_kernel(parts, *refs):
    refs[-1][...] = sum(r[...].astype(f32) for r in refs[:parts]).astype(bf16)


def near(parts, ties=()):
    return kernel_call(functools.partial(near_kernel, len(parts)), parts, [((ROWS, E), bf16)], ties=ties)[0]


def text_split_kernel(*refs):
    keep_ref, send_ref = refs[-2:]
    keep_ref[...] = sum(r[:HALF, :].astype(f32) for r in refs[:3])
    send_ref[...] = sum(r[HALF:, :].astype(f32) for r in refs[:3]).astype(bf16)


def image_split_kernel(half, *refs):
    keep_ref, send_ref = refs[-2:]
    for which, out_ref in ((half[0], keep_ref), (1 - half[0], send_ref)):
        rows = pl.ds(pl.multiple_of(which * HALF, HALF), HALF)
        out_ref[...] = sum(r[rows, :].astype(f32) for r in refs[:4]).astype(out_ref.dtype)


def backward(raw, grad):
    values = raw.astype(f32)
    inverse = lax.rsqrt(jnp.sum(values * values, axis=1, keepdims=True) + EPS)
    unit_values = values * inverse
    inner = jnp.sum(unit_values * grad, axis=1, keepdims=True)
    return ((grad - unit_values * inner) * inverse).astype(bf16)


def last_kernel(pos_ref, img_ref, txt_ref, i_ref, ir_ref, *refs):
    t_refs, (gi_ref, gt_ref) = refs[:2], refs[2:]
    rows = pl.ds(pl.multiple_of(pos_ref[0] * HALF, HALF), HALF)
    gi_ref[...] = backward(img_ref[rows, :], i_ref[...] + ir_ref[...].astype(f32))
    gt_ref[...] = backward(txt_ref[rows, :], sum(r[...].astype(f32) for r in t_refs))


def ring(axis, by):
    n = SIZES[AXES.index(axis)]
    return [(i, (i + by) % n) for i in range(n)]


def both_ways(value, axis):
    return lax.ppermute(value, axis, ring(axis, 1)), lax.ppermute(value, axis, ring(axis, -1))


def by_core(value, axis, by=1):
    n = SIZES[AXES.index(axis)]
    perm = [(i * 2 + c, (i + (1 - 2 * c) * by) % n * 2 + c) for i in range(n) for c in range(2)]
    return lax.ppermute(value, (axis, "c"), perm)


def swapped(value, axis, bit=1):
    n = SIZES[AXES.index(axis)]
    return lax.ppermute(value, axis, [(i, i ^ bit) for i in range(n)])


def cross_y(value):
    perm = []
    for yl in range(2):
        for c in range(2):
            for yh in range(2):
                perm.append(((yl * 2 + c) * 2 + yh, ((1 - yl) * 2 + c) * 2 + (yh ^ c)))
    return lax.ppermute(value, ("yl", "c", "yh"), perm)


def local(img_emb, txt_emb, pair_ids, log_scale, bias):
    yh, c = lax.axis_index("yh"), lax.axis_index("c")
    core = c.reshape(1).astype(jnp.int32)
    zero = jnp.zeros((1,), jnp.int32)
    pos = yh.reshape(1).astype(jnp.int32)
    temper = jnp.exp(log_scale[0])
    scalars = jnp.stack([temper, temper * LOG2E, bias[0] * LOG2E])
    t_own, tags = kernel_call(
        text_kernel, (pos, core, txt_emb, pair_ids.reshape(1, ROWS)), [((HALF, EX), bf16), ((ROWS, 128), bf16)]
    )
    t_yl = cross_y(t_own)
    (i_own,) = kernel_call(image_kernel, (scalars, img_emb, tags), [((ROWS, EX), bf16)])
    i_own = after(i_own, t_yl)
    i_low, i_high = both_ways(i_own, "z")
    i_own_s = swapped(i_own, "c")
    t_own = stacked(zero, t_own, t_yl)
    t_low, t_high = both_ways(t_own, "x")
    t_pass, i_pass = kernel_call(
        gather_gate, (core, t_low, t_high, i_low, i_high), [((ROWS, EX), bf16)] * 2
    )
    t_far, i_far = by_core(t_pass, "x"), by_core(i_pass, "z")
    i_low_s, i_high_s = swapped(i_low, "c"), swapped(i_high, "c")
    i_near, t_near, p_near, loss_a = logits(
        scalars, (i_own, i_own_s, i_low, i_low_s, i_high, i_high_s), (t_own, t_low, t_high)
    )
    i_far = after(i_far, loss_a, t_far)
    i_far_s = swapped(i_far, "c")
    t_far, p_cols, loss_b = logits(scalars, (), (t_far,), (i_near,))
    i_far, p_rows, loss_c = logits(scalars, (i_far, i_far_s), (), (), (t_near, t_far))
    losses, texts, images = (loss_a, loss_b, loss_c), (t_near, t_far), (i_near, i_far)
    far_s, far = image_grads(core, (1, 0), (p_rows, p_rows), texts, losses)
    (t_far,) = text_grads(core, ((0, 3),), (p_cols, p_rows), images, ties=(far,))
    t_got = by_core(t_far, "x")
    z_far, loss = kernel_call(
        far_kernel, (far, swapped(far_s, "c"), *losses), [((ROWS, E), bf16), ((8, 128), f32)], ties=(t_far,)
    )
    z_got = by_core(z_far, "z")
    near_parts, near_texts = (p_near, p_cols), (p_near, p_rows)
    two_s, one = image_grads(core, ((5, 3), (2, 4)), near_parts, texts, ties=(z_far,))
    (t_one,) = text_grads(core, (((1, 2), (1, 2)),), near_texts, images, ties=(one,))
    t_from_one = by_core(t_one, "x", -1)
    z_one = near((one, swapped(two_s, "c")), ties=(t_one,))
    z_from_one = by_core(z_one, "z", -1)
    one_s, two = image_grads(core, ((3, 5), (4, 2)), near_parts, texts, ties=(z_one,))
    (t_two,) = text_grads(core, (((2, 1), (2, 1)),), near_texts, images, ties=(two,))
    own_s, own = image_grads(core, (1, 0), near_parts, texts, ties=(t_two,))
    (t_own,) = text_grads(core, ((0, 0),), near_texts, images, ties=(own,))
    got_two, got_own = swapped(one_s, "c"), swapped(own_s, "c")
    t_two = near((t_two, t_got), ties=(z_got, z_from_one, t_from_one, t_own))
    z_two = near((two, got_two, z_got), ties=(t_got, z_from_one, t_from_one, t_own, got_own))
    t_from_two, z_from_two = by_core(t_two, "x"), by_core(z_two, "z")
    loss = after(loss, z_two, t_two)
    flips = [[(i, i ^ bits) for i in range(4)] for bits in (1, 2, 3)]
    loss = sum_of(loss, *[lax.ppermute(loss, ("yl", "yh"), perm) for perm in flips])
    half = (HALF, E)
    t_keep, t_send = kernel_call(
        text_split_kernel, (t_own, t_from_one, t_from_two), [(half, f32), (half, bf16)], ties=(loss,)
    )
    i_keep, i_send = kernel_call(
        image_split_kernel, (pos, own, got_own, z_from_one, z_from_two), [(half, f32), (half, bf16)], ties=(t_send,)
    )
    loss = after(loss, i_send)
    i_recv = swapped(i_send, "yh")
    t_recv = cross_y(t_send)
    for axis in ("x", "z"):
        loss = sum_of(loss, *[lax.ppermute(loss, axis, ring(axis, by)) for by in (1, -1, 2)])
    grad_image, grad_text = kernel_call(
        last_kernel, (pos, img_emb, txt_emb, i_keep, i_recv, t_keep, t_recv), [((HALF, E), bf16)] * 2
    )
    return (grad_image, grad_text, loss[0, :1] / (64 * ROWS))


def solution(mesh):
    fine = Mesh(mesh.devices.reshape(SIZES), AXES)
    group = ("z", "yl", "x", "c")
    return jax.shard_map(
        local,
        mesh=fine,
        in_specs=(P(group, None), P(group, None), P(group), P(), P()),
        out_specs=(P(AXES, None), P(AXES, None), P()),
        check_vma=False,
    )
```

```python
import functools

import jax
import jax.numpy as jnp
from jax import lax
from jax.experimental import pallas as pl
from jax.experimental.pallas import tpu as pltpu
from jax.sharding import Mesh
from jax.sharding import PartitionSpec as P

EPS = 1e-06
E = 1792
EX = E + 128
ROWS = 256
HALF = ROWS // 2
STEP = 2 * ROWS
LOG2E = 1.4426950408889634
VMEM = 56 << 20
f32 = jnp.float32
bf16 = jnp.bfloat16
AXES = ("z", "yl", "x", "c", "yh")
SIZES = (4, 2, 4, 2, 2)
NT = (((1,), (1,)), ((), ()))
NN = (((1,), (0,)), ((), ()))
TN = (((0,), (0,)), ((), ()))


def dot(a, b, dims):
    return lax.dot_general(a, b, dims, preferred_element_type=f32)


def tags_of(ids):
    n = ROWS
    eye = lax.broadcasted_iota(jnp.int32, (n, n), 0) == lax.broadcasted_iota(jnp.int32, (n, n), 1)
    hi = jnp.sum(jnp.where(eye, (ids >> 7).astype(f32), 0.0), axis=1, keepdims=True)
    lo = jnp.sum(jnp.where(eye, (ids & 127).astype(f32), 0.0), axis=1, keepdims=True)
    lane = lax.broadcasted_iota(jnp.int32, (n, 128), 1)
    return jnp.where(lane == 0, hi, jnp.where(lane == 1, lo, 0.0)).astype(bf16)


def unit(rows):
    values = rows.astype(f32)
    return (values * lax.rsqrt(jnp.sum(values * values, axis=1, keepdims=True) + EPS)).astype(bf16)


def text_kernel(pos_ref, core_ref, txt_ref, ids_ref, own_ref, tags_ref):
    del core_ref
    tags_ref[...] = tags_of(ids_ref[...])
    rows = pl.ds(pl.multiple_of(pos_ref[0] * HALF, HALF), HALF)
    own_ref[:, :E] = unit(txt_ref[rows, :])
    own_ref[:, E:] = tags_ref[rows, :]


def image_kernel(scalars_ref, img_ref, tags_ref, *refs):
    del scalars_ref
    out_ref = refs[-1]
    out_ref[:, :E] = unit(img_ref[...])
    out_ref[:, E:] = tags_ref[...]


VM = pl.BlockSpec(memory_space=pltpu.VMEM)
SM = pl.BlockSpec(memory_space=pltpu.SMEM)


def kernel_call(body, ins, outs, scratch=(), ties=(), aliases={}, limit=6 << 20):
    specs = [SM if x.ndim == 1 else VM for x in ins] + [pl.BlockSpec(memory_space=pl.ANY)] * len(ties)
    return pl.pallas_call(
        body,
        in_specs=specs,
        out_specs=[VM] * len(outs),
        out_shape=[jax.ShapeDtypeStruct(*o) for o in outs],
        scratch_shapes=list(scratch),
        input_output_aliases=dict(aliases),
        compiler_params=pltpu.CompilerParams(vmem_limit_bytes=limit),
        cost_estimate=pl.CostEstimate(flops=0, bytes_accessed=0, transcendentals=0),
    )(*ins, *ties)


def id_row(tags):
    lane = lax.broadcasted_iota(jnp.int32, (8, 128), 1)
    pick = jnp.where(lane == 0, 128.0, jnp.where(lane == 1, 1.0, 0.0)).astype(bf16)
    return dot(pick, tags, NT)


def id_col(tags):
    parts = tags[:, :2].astype(f32)
    return parts[:, 0:1] * 128.0 + parts[:, 1:2]


def pair_terms(products, same, temper, scale, shift):
    t = products * scale + shift
    e = jnp.exp2(jnp.where(same, -t, t))
    u = 1.0 + e
    r = pltpu.reciprocal(u, approx=True)
    r = r * (2.0 - u * r)
    coef = (jnp.where(same, -temper, temper) * (e * r)).astype(bf16)
    loss = jnp.log(u) + (e - (u - 1.0)) * r
    return coef, loss


def logits_kernel(n_i, n_t, old_i, old_t, *refs):
    refs = list(refs)
    sc = refs.pop(0)
    new_i, new_t = refs[:n_i], refs[n_i : n_i + n_t]
    refs = refs[n_i + n_t :]
    had_i, had_t = refs[:old_i], refs[old_i : old_i + old_t]
    outs, (coef_ref, loss_ref, trow, i_sem, t_sem) = refs[old_i + old_t : -5], refs[-5:]
    temper, scale, shift = sc[0], sc[1], sc[2]
    rows = outs[0] if new_i else had_i[0]
    for k, ref in enumerate(new_i):
        pltpu.make_async_copy(ref, rows.at[pl.ds(k * ROWS, ROWS)], i_sem.at[k]).start()
    cols, copies = [], []
    for k, ref in enumerate(new_t):
        copy = pltpu.make_async_copy(ref, outs[-1].at[pl.ds(k * ROWS, ROWS)], t_sem.at[k])
        copy.start()
        cols.append(ref)
        copies.append(copy)
    for ref in had_t:
        cols += [ref.at[pl.ds(k, ROWS)] for k in range(0, ref.shape[0], ROWS)]
    loss_ref[...] = jnp.zeros_like(loss_ref)
    for j, text in enumerate(cols):
        trow[j] = id_row(text[:, E:])

    def step(image, here):
        column = id_col(image[:, E:])
        for j, text in enumerate(cols):
            products = dot(image[:, :E], text[:, :E], NT)
            coef, loss = pair_terms(products, column == trow[j, 0:1], temper, scale, shift)
            coef_ref[here, j * ROWS : (j + 1) * ROWS] = coef
            loss_ref[...] += jnp.sum(loss.reshape(image.shape[0] // 8, 8, ROWS), axis=0)

    def copied_step(k, carry):
        here = pl.ds(pl.multiple_of(k * STEP, STEP), STEP)
        for part in range(STEP // ROWS):
            piece = rows.at[pl.ds(pl.multiple_of(k * STEP + part * ROWS, ROWS), ROWS)]
            pltpu.make_async_copy(piece, piece, i_sem.at[k * (STEP // ROWS) + part]).wait()
        step(rows.at[here], here)
        return carry

    if n_i > 2:
        lax.fori_loop(0, n_i * ROWS // STEP, copied_step, 0)
    elif n_i:
        for k, ref in enumerate(new_i):
            step(ref, pl.ds(k * ROWS, ROWS))
        for k in range(n_i):
            piece = rows.at[pl.ds(k * ROWS, ROWS)]
            pltpu.make_async_copy(piece, piece, i_sem.at[k]).wait()
    else:
        for k in range(0, rows.shape[0], STEP):
            step(rows.at[pl.ds(k, STEP)], pl.ds(k, STEP))
    for copy in copies:
        copy.wait()


def logits(scalars, new_i=(), new_t=(), old_i=(), old_t=()):
    total = [sum(x.shape[0] for x in group) for group in (new_i, new_t, old_i, old_t)]
    rows, cols = total[0] + total[2], total[1] + total[3]
    return kernel_call(
        functools.partial(logits_kernel, len(new_i), len(new_t), len(old_i), len(old_t)),
        (scalars, *new_i, *new_t, *old_i, *old_t),
        [((n, EX), bf16) for n in total[:2] if n] + [((rows, cols), bf16), ((8, ROWS), f32)],
        scratch=[pltpu.VMEM((cols // ROWS, 8, ROWS), f32), pltpu.SemaphoreType.DMA((len(new_i) or 1,)), pltpu.SemaphoreType.DMA((len(new_t) or 1,))],
        limit=12 << 20,
    )


def block(core_ref, k):
    start = jnp.where(core_ref[0] == 0, k[0], k[1]) if isinstance(k, tuple) else k
    return pl.ds(pl.multiple_of(start * ROWS, ROWS), ROWS)


def image_grads_kernel(blocks, parts, losses, ties, core_ref, *refs):
    coefs, texts = refs[:parts], refs[parts : 2 * parts]
    losses, outs = refs[2 * parts : 2 * parts + losses], refs[2 * parts + losses + ties :]
    for out_ref, k in zip(outs, blocks):
        rows = block(core_ref, k)
        at, grad = 0, None
        for n, text in enumerate(texts):
            coef = coefs[n][rows, :] if coefs[n].shape[1] == text.shape[0] else coefs[n][rows, at : at + text.shape[0]]
            part = dot(coef, text[:, :E], NN)
            grad = part if grad is None else grad + part
            at += text.shape[0]
        out_ref[:ROWS, :] = grad.astype(bf16)
    if losses:
        put(outs[0], jnp.sum(sum(r[...] for r in losses)))


def text_grads_kernel(blocks, parts, ties, core_ref, *refs):
    coefs, images = refs[:parts], refs[parts : 2 * parts]
    for out_ref, ks in zip(refs[2 * parts + ties :], blocks):
        sums = [dot(c[:, block(core_ref, k)], i[:, :E], TN) for c, i, k in zip(coefs, images, ks)]
        out_ref[...] = sum(sums[1:], sums[0]).astype(bf16)


def image_grads(core, blocks, coefs, texts, losses=(), ties=()):
    first = ((ROWS + 16 if losses else ROWS, E), bf16)
    return kernel_call(
        functools.partial(image_grads_kernel, blocks, len(texts), len(losses), len(ties)),
        (core, *coefs, *texts, *losses),
        [first] + [((ROWS, E), bf16)] * (len(blocks) - 1),
        ties=ties,
        limit=10 << 20,
    )


def text_grads(core, blocks, coefs, images, ties=()):
    return kernel_call(
        functools.partial(text_grads_kernel, blocks, len(images), len(ties)),
        (core, *coefs, *images),
        [((ROWS, E), bf16)] * len(blocks),
        ties=ties,
        limit=10 << 20,
    )


def sum_kernel(*refs):
    refs[-1][...] = sum(r[...] for r in refs[:-1])


def sum_of(*parts):
    return kernel_call(sum_kernel, parts, [(parts[0].shape, parts[0].dtype)])[0]


def far_kernel(own_ref, got_ref, *refs):
    losses, (out_ref, loss_ref) = refs[:3], refs[-2:]
    out_ref[...] = (own_ref[...].astype(f32) + got_ref[:ROWS, :].astype(f32)).astype(bf16)
    loss_ref[...] = jnp.full((8, 128), jnp.sum(sum(r[...] for r in losses)) + take(got_ref), f32)


def stack_kernel(at_ref, a_ref, b_ref, *refs):
    n = a_ref.shape[0]
    out_ref = refs[-1]
    out_ref[pl.ds(pl.multiple_of(at_ref[0] * n, n), n), :] = a_ref[...]
    out_ref[pl.ds(pl.multiple_of((1 - at_ref[0]) * n, n), n), :] = b_ref[...]


def stacked(at, a, b, ties=()):
    return kernel_call(stack_kernel, (at, a, b), [((2 * a.shape[0], a.shape[1]), bf16)], ties=ties)[0]


def copy_kernel(in_ref, *refs):
    refs[-1][...] = in_ref[...]


def after(value, *ties):
    return kernel_call(copy_kernel, (value,), [(value.shape, value.dtype)], ties=ties)[0]


def put(ref, number):
    lane = lax.broadcasted_iota(jnp.int32, (16, 128), 1)
    rest = jnp.full((16, 128), number, f32)
    parts = []
    for _ in range(3):
        parts.append(rest.astype(bf16).astype(f32))
        rest = rest - parts[-1]
    value = jnp.where(lane == 0, parts[0], jnp.where(lane == 1, parts[1], jnp.where(lane == 2, parts[2], 0.0)))
    ref[ROWS:, :128] = value.astype(bf16)
    ref[ROWS:, 128:] = jnp.zeros((16, E - 128), bf16)


def take(ref):
    lane = lax.broadcasted_iota(jnp.int32, (16, 128), 1)
    row = lax.broadcasted_iota(jnp.int32, (16, 128), 0)
    return jnp.sum(jnp.where((lane < 3) & (row == 0), ref[ROWS:, :128].astype(f32), 0.0))


def gather_gate(core, t_low, t_high, i_low, i_high, t_out, i_out):
    for k, (text, image) in enumerate(((t_low, i_low), (t_high, i_high))):

        @pl.when(core[0] == k)
        def _():
            t_out[...], i_out[...] = text[...], image[...]


def near_kernel(parts, *refs):
    refs[-1][...] = sum(r[...].astype(f32) for r in refs[:parts]).astype(bf16)


def near(parts, ties=()):
    return kernel_call(functools.partial(near_kernel, len(parts)), parts, [((ROWS, E), bf16)], ties=ties)[0]


def text_split_kernel(*refs):
    keep_ref, send_ref = refs[-2:]
    keep_ref[...] = sum(r[:HALF, :].astype(f32) for r in refs[:3])
    send_ref[...] = sum(r[HALF:, :].astype(f32) for r in refs[:3]).astype(bf16)


def image_split_kernel(half, *refs):
    keep_ref, send_ref = refs[-2:]
    for which, out_ref in ((half[0], keep_ref), (1 - half[0], send_ref)):
        rows = pl.ds(pl.multiple_of(which * HALF, HALF), HALF)
        out_ref[...] = sum(r[rows, :].astype(f32) for r in refs[:4]).astype(out_ref.dtype)


def backward(raw, grad):
    values = raw.astype(f32)
    inverse = lax.rsqrt(jnp.sum(values * values, axis=1, keepdims=True) + EPS)
    unit_values = values * inverse
    inner = jnp.sum(unit_values * grad, axis=1, keepdims=True)
    return ((grad - unit_values * inner) * inverse).astype(bf16)


def last_kernel(pos_ref, img_ref, txt_ref, i_ref, ir_ref, *refs):
    t_refs, (gi_ref, gt_ref) = refs[:2], refs[2:]
    rows = pl.ds(pl.multiple_of(pos_ref[0] * HALF, HALF), HALF)
    gi_ref[...] = backward(img_ref[rows, :], i_ref[...] + ir_ref[...].astype(f32))
    gt_ref[...] = backward(txt_ref[rows, :], sum(r[...].astype(f32) for r in t_refs))


def ring(axis, by):
    n = SIZES[AXES.index(axis)]
    return [(i, (i + by) % n) for i in range(n)]


def both_ways(value, axis):
    return lax.ppermute(value, axis, ring(axis, 1)), lax.ppermute(value, axis, ring(axis, -1))


def by_core(value, axis, by=1):
    n = SIZES[AXES.index(axis)]
    perm = [(i * 2 + c, (i + (1 - 2 * c) * by) % n * 2 + c) for i in range(n) for c in range(2)]
    return lax.ppermute(value, (axis, "c"), perm)


def swapped(value, axis, bit=1):
    n = SIZES[AXES.index(axis)]
    return lax.ppermute(value, axis, [(i, i ^ bit) for i in range(n)])


def cross_y(value):
    perm = []
    for yl in range(2):
        for c in range(2):
            for yh in range(2):
                perm.append(((yl * 2 + c) * 2 + yh, ((1 - yl) * 2 + c) * 2 + (yh ^ c)))
    return lax.ppermute(value, ("yl", "c", "yh"), perm)


def local(img_emb, txt_emb, pair_ids, log_scale, bias):
    yh, c = lax.axis_index("yh"), lax.axis_index("c")
    core = c.reshape(1).astype(jnp.int32)
    zero = jnp.zeros((1,), jnp.int32)
    pos = yh.reshape(1).astype(jnp.int32)
    temper = jnp.exp(log_scale[0])
    scalars = jnp.stack([temper, temper * LOG2E, bias[0] * LOG2E])
    t_own, tags = kernel_call(
        text_kernel, (pos, core, txt_emb, pair_ids.reshape(1, ROWS)), [((HALF, EX), bf16), ((ROWS, 128), bf16)]
    )
    t_yl = cross_y(t_own)
    (i_own,) = kernel_call(image_kernel, (scalars, img_emb, tags), [((ROWS, EX), bf16)])
    i_own = after(i_own, t_yl)
    i_low, i_high = both_ways(i_own, "z")
    i_own_s = swapped(i_own, "c")
    t_own = stacked(zero, t_own, t_yl)
    t_low, t_high = both_ways(t_own, "x")
    t_pass, i_pass = kernel_call(
        gather_gate, (core, t_low, t_high, i_low, i_high), [((ROWS, EX), bf16)] * 2
    )
    t_far, i_far = by_core(t_pass, "x"), by_core(i_pass, "z")
    i_low_s, i_high_s = swapped(i_low, "c"), swapped(i_high, "c")
    i_near, t_near, p_near, loss_a = logits(
        scalars, (i_own, i_own_s, i_low, i_low_s, i_high, i_high_s), (t_own, t_low, t_high)
    )
    i_far = after(i_far, loss_a, t_far)
    i_far_s = swapped(i_far, "c")
    t_far, p_cols, loss_b = logits(scalars, (), (t_far,), (i_near,))
    i_far, p_rows, loss_c = logits(scalars, (i_far, i_far_s), (), (), (t_near, t_far))
    losses, texts, images = (loss_a, loss_b, loss_c), (t_near, t_far), (i_near, i_far)
    far_s, far = image_grads(core, (1, 0), (p_rows, p_rows), texts, losses)
    near_parts, near_texts = (p_near, p_cols), (p_near, p_rows)
    two_s, one = image_grads(core, ((5, 3), (2, 4)), near_parts, texts, ties=(far,))
    (t_far,) = text_grads(core, ((0, 3),), (p_cols, p_rows), images, ties=(one,))
    t_got = by_core(t_far, "x")
    z_far, loss = kernel_call(
        far_kernel, (far, swapped(far_s, "c"), *losses), [((ROWS, E), bf16), ((8, 128), f32)], ties=(t_far,)
    )
    z_got = by_core(z_far, "z")
    z_one = near((one, swapped(two_s, "c")), ties=(z_far,))
    z_from_one = by_core(z_one, "z", -1)
    (t_one,) = text_grads(core, (((1, 2), (1, 2)),), near_texts, images, ties=(z_one,))
    t_from_one = by_core(t_one, "x", -1)
    one_s, two = image_grads(core, ((3, 5), (4, 2)), near_parts, texts, ties=(t_one,))
    (t_two,) = text_grads(core, (((2, 1), (2, 1)),), near_texts, images, ties=(two,))
    own_s, own = image_grads(core, (1, 0), near_parts, texts, ties=(t_two,))
    (t_own,) = text_grads(core, ((0, 0),), near_texts, images, ties=(own,))
    got_two, got_own = swapped(one_s, "c"), swapped(own_s, "c")
    t_two = near((t_two, t_got), ties=(z_got, z_from_one, t_from_one, t_own))
    z_two = near((two, got_two, z_got), ties=(t_got, z_from_one, t_from_one, t_own, got_own))
    t_from_two, z_from_two = by_core(t_two, "x"), by_core(z_two, "z")
    loss = after(loss, z_two, t_two)
    flips = [[(i, i ^ bits) for i in range(4)] for bits in (1, 2, 3)]
    loss = sum_of(loss, *[lax.ppermute(loss, ("yl", "yh"), perm) for perm in flips])
    half = (HALF, E)
    t_keep, t_send = kernel_call(
        text_split_kernel, (t_own, t_from_one, t_from_two), [(half, f32), (half, bf16)], ties=(loss,)
    )
    i_keep, i_send = kernel_call(
        image_split_kernel, (pos, own, got_own, z_from_one, z_from_two), [(half, f32), (half, bf16)], ties=(t_send,)
    )
    loss = after(loss, i_send)
    i_recv = swapped(i_send, "yh")
    t_recv = cross_y(t_send)
    for axis in ("x", "z"):
        loss = sum_of(loss, *[lax.ppermute(loss, axis, ring(axis, by)) for by in (1, -1, 2)])
    grad_image, grad_text = kernel_call(
        last_kernel, (pos, img_emb, txt_emb, i_keep, i_recv, t_keep, t_recv), [((HALF, E), bf16)] * 2
    )
    return (grad_image, grad_text, loss[0, :1] / (64 * ROWS))


def solution(mesh):
    fine = Mesh(mesh.devices.reshape(SIZES), AXES)
    group = ("z", "yl", "x", "c")
    return jax.shard_map(
        local,
        mesh=fine,
        in_specs=(P(group, None), P(group, None), P(group), P(), P()),
        out_specs=(P(AXES, None), P(AXES, None), P()),
        check_vma=False,
    )
```
